256 devices in a mesh: req: 8 (over y, core), chan: 32 (over z, x).
Axes of the slice: x: 4, y: 4, z: 8, core: 2. Of those that a mesh axis runs over, the one named last changes fastest.
Arguments:
- hidden: bfloat16 [1024, 8192], P('req', 'chan'), parts along dimension 0, may hold values from -200 to 200
- norm_gain: bfloat16 [8192], P('chan'), may hold values from 0.099609375 to 1.8984375
- in_weight: bfloat16 [8192, 2, 8192], P(None, None, 'chan'), may hold values from -0.0625 to 0.0625
- conv_weight: float32 [4, 8192], P(None, 'chan'), may hold values from -3 to 3
- conv_bias: float32 [8192], P('chan'), may hold values from -3 to 3
- x_proj_weight: bfloat16 [8192, 544], P('chan'), may hold values from -0.0625 to 0.0625
- dt_norm_gain: float32 [512], replicated, may hold values from 0.1 to 1.9
- b_norm_gain: float32 [16], replicated, may hold values from 0.1 to 1.9
- c_norm_gain: float32 [16], replicated, may hold values from 0.1 to 1.9
- dt_weight: bfloat16 [512, 8192], P(None, 'chan'), may hold values from -0.25 to 0.25
- dt_bias: float32 [8192], P('chan'), may hold values from -2.3 to 0.5
- decay_log: float32 [16, 8192], P(None, 'chan'), may hold values from 0 to 2.77
- skip_gain: float32 [8192], P('chan'), may hold values from 0.5 to 1.5
- conv_state: bfloat16 [1024, 3, 8192], P('req', None, 'chan'), parts along dimension 0, may hold values from -6 to 6
- ssm_state: bfloat16 [1024, 16, 8192], P('req', None, 'chan'), parts along dimension 0, may hold values from -6 to 6
Outputs:
- gated_output: bfloat16 [1024, 8192], P('req', 'chan'), parts along dimension 0
- next_conv_state: bfloat16 [1024, 3, 8192], P('req', None, 'chan'), parts along dimension 0
- next_ssm_state: bfloat16 [1024, 16, 8192], P('req', None, 'chan'), parts along dimension 0
The draws below stay inside these ranges and needn't reach their ends.
There are 8 independent parts, one for each index of `req`. The reference program is written for one: setup_inputs(seed, part) draws one part's arguments, and reference() takes and returns one part's arrays. A program takes and returns all parts, laid end to end along the dimension named above; an argument that names none is the same for every part. Nothing has to cross between parts.
All inputs are finite; a program needn't handle non-finite values.
Results may differ from the reference program's by a relative error of at most 0.0113.
Values may be sent and summed in bfloat16 or wider, within the bound.
A program may use at most 64 MiB of HBM per device.

```python
import math
import jax
import jax.numpy as jnp
from jax import lax

D = 8192
N = 16
DT_RANK = 512
CONV = 4
INNER = 8192
REQ = 128


def draw_hidden(key, part):
    key = jax.random.fold_in(key, 11)
    row_key, base_key = jax.random.split(key)
    column = jnp.arange(D, dtype=jnp.float32) / D
    row_scale = jnp.exp(jax.random.uniform(row_key, (REQ, 1), jnp.float32) * math.log(10.0))
    base = jnp.clip(jax.random.normal(base_key, (REQ, D), jnp.float32), -4.0, 4.0)
    column_scale = jnp.exp(column * math.log(10.0))
    return (0.5 * base * row_scale * column_scale[None, :]).astype(jnp.bfloat16)


def block_levels(own_key, shape, pieces, least, largest):
    gain, own = 1.0, jax.random.fold_in(own_key, 6)
    for position, blocks in pieces:
        draws = jnp.exp(jax.random.uniform(jax.random.fold_in(own, position), (blocks,), jnp.float32, least / len(pieces), largest / len(pieces)))
        gain = gain * jnp.repeat(draws, shape[position] // blocks).reshape([-1 if axis == position else 1 for axis in range(len(shape))])
    return gain


def gaussian(stream_key, extent, spread, reach, cuts=(), kind=jnp.bfloat16):
    values = jax.random.normal(stream_key, extent, jnp.float32) * spread
    if len(cuts) > 0:
        values = block_levels(stream_key, extent, cuts, -0.22, 0.18) * values
    return jnp.clip(values, min=-reach, max=reach).astype(kind)


def setup_inputs(seed: int = 0, part: int = 0) -> dict:
    key_list = jax.random.split(jax.random.key(seed), 16)
    part_splits = jax.random.split(jax.random.fold_in(key_list[15], part), 16)
    return {
        "hidden": draw_hidden(jax.random.fold_in(jax.random.fold_in(key_list[15], part), 71), part),
        "norm_gain": jnp.clip(1.0 + 0.18 * jax.random.normal(key_list[1], (D,), jnp.float32), 0.099609375, 1.8984375).astype(jnp.bfloat16),
        "in_weight": gaussian(key_list[2], (D, 2, INNER), D ** -0.5, 0.0625, ((2, 32),)),
        "conv_weight": gaussian(key_list[3], (CONV, INNER), 0.5, 3.0, ((1, 32),), jnp.float32),
        "conv_bias": gaussian(key_list[4], (INNER,), 0.5, 3.0, ((0, 32),), jnp.float32),
        "x_proj_weight": gaussian(key_list[5], (INNER, DT_RANK + 2 * N), INNER ** -0.5, 0.0625, ((0, 32),)),
        "dt_norm_gain": jnp.clip(1.0 + 0.18 * jax.random.normal(key_list[6], (DT_RANK,), jnp.float32), 0.1, 1.9),
        "b_norm_gain": jnp.clip(1.0 + 0.18 * jax.random.normal(key_list[7], (N,), jnp.float32), 0.1, 1.9),
        "c_norm_gain": jnp.clip(1.0 + 0.18 * jax.random.normal(key_list[8], (N,), jnp.float32), 0.1, 1.9),
        "dt_weight": gaussian(key_list[9], (DT_RANK, INNER), DT_RANK ** -0.5, 0.25, ((1, 32),)),
        "dt_bias": jnp.clip(-2.3 + 2.8 * jax.random.uniform(key_list[10], (INNER,), jnp.float32) ** block_levels(key_list[10], (INNER,), ((0, 32),), -0.2, 0.2), -2.3, 0.5),
        "decay_log": jnp.clip(2.77 * jax.random.uniform(key_list[11], (N, INNER), jnp.float32) ** block_levels(key_list[11], (N, INNER), ((1, 32),), -0.2, 0.2), 0.0, 2.77),
        "skip_gain": jnp.clip(0.5 + 1.0 * jax.random.uniform(key_list[12], (INNER,), jnp.float32) ** block_levels(key_list[12], (INNER,), ((0, 32),), -0.2, 0.2), 0.5, 1.5),
        "conv_state": gaussian(part_splits[13], (REQ, CONV - 1, INNER), 1.0, 6.0, ((2, 32),)),
        "ssm_state": gaussian(part_splits[14], (REQ, N, INNER), 1.0, 6.0, ((2, 32),)),
    }


def rms_scale(values, epsilon):
    return values * lax.rsqrt(lax.optimization_barrier(jnp.mean(values * values, axis=-1, keepdims=True)) + epsilon)

def reference(hidden, norm_gain, in_weight, conv_weight, conv_bias, x_proj_weight, dt_norm_gain, b_norm_gain, c_norm_gain, dt_weight, dt_bias, decay_log, skip_gain, conv_state, ssm_state):
    widened = hidden.astype(jnp.float32)
    normed = (rms_scale(widened, 1e-05) * norm_gain.astype(jnp.float32)).astype(jnp.bfloat16)
    flat_weight = in_weight.reshape(D, 2 * INNER)
    mixed = jnp.dot(normed, flat_weight, preferred_element_type=jnp.float32).astype(jnp.bfloat16)
    new_inputs = mixed[:, :INNER]
    gate_half = mixed[:, INNER:]
    window = jnp.concatenate([conv_state, new_inputs[:, None, :]], axis=1)
    next_conv = window[:, 1:, :]
    conv_out = lax.optimization_barrier(jnp.sum(window.astype(jnp.float32) * conv_weight[None], axis=1)) + conv_bias
    conv_act = jax.nn.silu(conv_out).astype(jnp.bfloat16)
    projected = jnp.dot(conv_act, x_proj_weight, preferred_element_type=jnp.float32)
    step_normed = (rms_scale(projected[:, :DT_RANK], 1e-06) * dt_norm_gain).astype(jnp.bfloat16)
    b_values = rms_scale(projected[:, DT_RANK:DT_RANK + N], 1e-06) * b_norm_gain
    c_values = rms_scale(projected[:, DT_RANK + N:], 1e-06) * c_norm_gain
    step_size = jax.nn.softplus(jnp.dot(step_normed, dt_weight, preferred_element_type=jnp.float32) + dt_bias)
    decay_rates = jnp.exp(decay_log)
    decay_factor = jnp.exp(-step_size[:, None, :] * decay_rates[None])
    act_wide = conv_act.astype(jnp.float32)
    new_state = decay_factor * ssm_state.astype(jnp.float32) + (step_size * act_wide)[:, None, :] * b_values[:, :, None]
    mixed_out = lax.optimization_barrier(jnp.sum(new_state * c_values[:, :, None], axis=1)) + skip_gain * act_wide
    output = (mixed_out * jax.nn.silu(gate_half.astype(jnp.float32))).astype(jnp.bfloat16)
    return (output, next_conv, new_state.astype(jnp.bfloat16))
```

```python
import jax
import jax.numpy as jnp
from jax import lax
from jax.experimental import pallas as pl
from jax.experimental.pallas import tpu as pltpu
from jax.sharding import PartitionSpec as P

D = 8192
N = 16
DT_RANK = 512
ZS = 8
XS = 4
DEVS = 32
REQ = 128
LOC = 256
MESH = pl.DeviceIdType.MESH
F32 = jnp.float32
BF16 = jnp.bfloat16

OWN = [
    (0, 0, 1), (0, 0, -1), (0, 1, 0), (0, -1, 0), (0, 0, 2),
    (1, 1, 0), (1, -1, 0), (1, 0, 1), (1, 0, -1), (1, 2, 0), (1, -2, 0), (1, 0, 2),
]


def passes():
    along_x = [(0, 1), (0, -1), (0, 2)]
    up, down = [(1, 0)], [(-1, 0)]
    order = [
        ((0, 0, -1), up + down), ((0, 0, 1), up + down), ((0, -1, 0), up), ((0, 1, 0), down),
        ((1, -1, 0), along_x), ((1, 1, 0), along_x), ((1, 0, -1), []), ((1, 0, 1), []),
        ((0, 0, 2), up + down),
        ((1, -2, 0), [(1, 0), (2, 0)] + along_x), ((1, 2, 0), [(-1, 0)] + along_x), ((1, 0, 2), []),
        ((0, -1, -1), up), ((0, 1, -1), down), ((0, -1, 1), up), ((0, 1, 1), down),
        ((1, -1, -1), []), ((1, -1, 1), []),
        ((0, -2, 0), [(1, 0), (2, 0)]), ((0, 2, 0), down),
        ((1, 1, -1), []), ((1, 1, 1), []),
        ((0, -1, 2), up), ((0, 1, 2), down),
        ((1, -3, 0), along_x), ((1, 3, 0), along_x),
        ((1, -1, 2), []), ((1, -2, -1), []), ((1, -2, 1), []),
        ((0, 2, -1), down), ((0, -2, -1), [(1, 0), (2, 0)]), ((1, 2, -1), []), ((0, 2, 1), [(-1, 0), (-2, 0)]),
        ((1, 2, 1), []),
        ((1, 4, 0), along_x), ((0, 3, 0), []), ((1, 1, 2), []), ((0, -2, 1), up), ((1, -2, 2), []),
        ((0, 2, 2), [(-1, 0), (-2, 0)]), ((1, 2, 2), []), ((0, -3, 0), []),
        ((1, -3, -1), []), ((1, -3, 1), []), ((0, 3, -1), []), ((1, 3, -1), []), ((1, 3, 1), []),
        ((0, -2, 2), up), ((0, 3, 1), []), ((0, 4, 0), []), ((1, -3, 2), []), ((1, 4, -1), []), ((1, 4, 1), []),
        ((0, -3, -1), []), ((0, 4, 1), []), ((1, 3, 2), []), ((0, 3, 2), []), ((1, 4, 2), []),
        ((0, -3, 1), []), ((0, 4, -1), []), ((0, 4, 2), []), ((0, -3, 2), []),
    ]
    return order


def gather_kernel(
    hidden, gain, weight_hbm, conv_weight, conv_bias, proj, conv_state,
    act_out, gate_out, conv_out, step_out, bc_out,
    raw, wide, ready, units, total, squares_x, squares_z, part, part_bc, got, got_bc,
    weight_sem, recv_sem, send_sem, sq_sem, sum_sem, out_sem,
):
    req = lax.axis_index("req")
    me = lax.axis_index("chan")
    mz = me // XS
    mx = lax.rem(me, XS)

    def place(dz, dx):
        return lax.rem(mz + dz + ZS, ZS) * XS + lax.rem(mx + dx + XS, XS)

    weight_copies = [
        pltpu.make_async_copy(
            weight_hbm.at[pl.ds(i * 4096, 4096)], raw.at[pl.ds(i * 4096, 4096)], weight_sem.at[i]
        )
        for i in range(8)
    ]
    for copy in weight_copies:
        copy.start()

    greeted = [(1, 0), (-1, 0), (2, 0), (-2, 0), (0, 1), (0, -1), (0, 2)]
    barrier = pltpu.get_barrier_semaphore()
    for dz, dx in greeted:
        pl.semaphore_signal(barrier, inc=1, device_id=(req, place(dz, dx)), device_id_type=MESH)

    widened = hidden[...].astype(F32)
    scaled = (widened * gain[...].astype(F32)).astype(BF16)
    units[0, pl.ds(me, 1)] = scaled[None, :, :128]
    units[1, pl.ds(me, 1)] = scaled[None, :, 128:]
    square_row = lax.dot_general(
        jnp.ones((8, LOC), F32), widened * widened, (((1,), (1,)), ((), ())),
        precision=lax.Precision.HIGHEST, preferred_element_type=F32,
    )
    squares_x[pl.ds(mx, 1)] = square_row[None, :1]

    pl.semaphore_wait(barrier, len(greeted))

    def push(half, dz, dx, hz, hx):
        owner = place(dz, dx)
        pltpu.make_async_remote_copy(
            units.at[half, owner], units.at[half, owner], send_sem.at[half],
            recv_sem.at[half, (dz - hz) % ZS, (dx - hx) % XS],
            device_id=(req, place(hz, hx)), device_id_type=MESH,
        ).start()

    def await_unit(half, dz, dx):
        owner = place(dz, dx)
        pltpu.make_async_copy(
            units.at[half, owner], units.at[half, owner], recv_sem.at[half, dz % ZS, dx % XS]
        ).wait()

    for half, hz, hx in OWN:
        push(half, 0, 0, hz, hx)
    for dx in (1, -1, 2):
        pltpu.make_async_remote_copy(
            squares_x.at[mx], squares_x.at[mx], sq_sem.at[0], sq_sem.at[1],
            device_id=(req, place(0, dx)), device_id_type=MESH,
        ).start()

    def convert(index, _):
        wide[...] = raw[pl.ds(pl.multiple_of(index * 1024, 1024), 1024), :].astype(F32)
        for side in range(2):
            for tile in range(2):
                column = side * 256 + tile * 128
                ready[pl.ds(pl.multiple_of(index * 256, 256), 256), column : column + 128] = wide[
                    pl.ds(2 * tile + side, 256, stride=4), :
                ].astype(BF16)
        return 0

    def multiply(dz, dx, first=False):
        owner = place(dz, dx)
        left = jnp.concatenate([units[0, owner], units[1, owner]], axis=1)
        product = jnp.dot(
            left, ready[pl.ds(pl.multiple_of(owner * 256, 256), 256), :], preferred_element_type=F32
        )
        total[...] = product if first else total[...] + product

    converted = 0

    def convert_to(count):
        nonlocal converted
        while converted < count:
            if converted % 4 == 0:
                weight_copies[converted // 4].wait()
            last = min(count, converted // 4 * 4 + 4)
            lax.fori_loop(converted, last, convert, 0)
            converted = last

    convert_to(8)
    arrived = {}
    pending = []
    started = False
    column = 0
    order = passes()
    for step, ((half, dz, dx), hops) in enumerate(order):
        await_unit(half, dz, dx)
        for hz, hx in hops:
            push(half, dz, dx, hz, hx)
        arrived[(dz, dx)] = arrived.get((dz, dx), 0) + 1
        if arrived[(dz, dx)] == 2:
            pending.append((dz, dx))
        if dx == 0 and half == 1:
            column += 1
            if column == 7:
                pltpu.make_async_copy(
                    squares_x.at[pl.ds(0, 3)], squares_x.at[pl.ds(0, 3)], sq_sem.at[1]
                ).wait()
                squares_z[pl.ds(mz, 1)] = jnp.sum(squares_x[...], axis=0, keepdims=True)
                for hz in (1, -1, 2, -2, 3, -3, 4):
                    pltpu.make_async_remote_copy(
                        squares_z.at[mz], squares_z.at[mz], sq_sem.at[2], sq_sem.at[3],
                        device_id=(req, place(hz, 0)), device_id_type=MESH,
                    ).start()
        if converted < DEVS:
            convert_to(min(DEVS, converted + 2))
        elif pending:
            if not started:
                multiply(0, 0, True)
                started = True
            multiply(*pending.pop(0))
    while pending:
        multiply(*pending.pop(0))

    pltpu.make_async_copy(squares_z.at[pl.ds(0, 7)], squares_z.at[pl.ds(0, 7)], sq_sem.at[3]).wait()
    row = jnp.sum(squares_z[...], axis=0)
    inverse_row = lax.rsqrt(row / D + 1e-05)
    inverse = jnp.transpose(jnp.broadcast_to(inverse_row, (128, 128)))
    mixed = [
        (total[:, i * 128 : i * 128 + 128] * inverse).astype(BF16) for i in range(4)
    ]
    new_inputs = jnp.concatenate(mixed[:2], axis=1)
    gate_out[...] = jnp.concatenate(mixed[2:], axis=1)
    conv_out[0] = conv_state[1]
    conv_out[1] = conv_state[2]
    conv_out[2] = new_inputs
    window = conv_state[0].astype(F32) * conv_weight[0:1]
    window += conv_state[1].astype(F32) * conv_weight[1:2]
    window += conv_state[2].astype(F32) * conv_weight[2:3]
    window += new_inputs.astype(F32) * conv_weight[3:4]
    window += conv_bias[...]
    act = (window * jax.nn.sigmoid(window)).astype(BF16)
    act_out[...] = act
    projected = lax.dot_general(
        proj[...], act, (((1,), (1,)), ((), ())), preferred_element_type=F32
    )
    part[...] = projected[:DT_RANK].astype(BF16)
    for i in range(2 * N):
        part_bc[i] = projected[DT_RANK + i : DT_RANK + i + 1]

    def rows(index):
        return pl.ds(pl.multiple_of(index * 16, 16), 16)

    def spread(i, _):
        peer = lax.rem(me + i, DEVS)
        pltpu.make_async_remote_copy(
            part.at[rows(peer)], got.at[rows(me)], sum_sem.at[0], sum_sem.at[1],
            device_id=(req, peer), device_id_type=MESH,
        ).start()
        pltpu.make_async_remote_copy(
            part_bc.at[peer], got_bc.at[me], sum_sem.at[2], sum_sem.at[3],
            device_id=(req, peer), device_id_type=MESH,
        ).start()
        return 0

    lax.fori_loop(1, DEVS, spread, 0)
    got[rows(me), :] = part[rows(me), :]
    got_bc[pl.ds(me, 1)] = part_bc[pl.ds(me, 1)]

    some, some_bc = pl.ds(0, 31 * 16), pl.ds(0, 31)
    pltpu.make_async_copy(got.at[some], got.at[some], sum_sem.at[1]).wait()
    pltpu.make_async_copy(got_bc.at[some_bc], got_bc.at[some_bc], sum_sem.at[3]).wait()
    step = got[0:16].astype(F32)
    for i in range(1, DEVS):
        step += got[i * 16 : i * 16 + 16].astype(F32)
    step_out[rows(me), :] = step.astype(BF16)
    bc_out[pl.ds(me, 1)] = jnp.sum(got_bc[...], axis=0, keepdims=True)

    def share(i, _):
        peer = lax.rem(me + i, DEVS)
        pltpu.make_async_remote_copy(
            step_out.at[rows(me)], step_out.at[rows(me)], out_sem.at[0], out_sem.at[1],
            device_id=(req, peer), device_id_type=MESH,
        ).start()
        pltpu.make_async_remote_copy(
            bc_out.at[me], bc_out.at[me], out_sem.at[2], out_sem.at[3],
            device_id=(req, peer), device_id_type=MESH,
        ).start()
        return 0

    lax.fori_loop(1, DEVS, share, 0)
    for half in range(2):
        pltpu.make_async_copy(
            units.at[half, pl.ds(0, 31)], units.at[half, pl.ds(0, 31)], send_sem.at[half]
        ).wait()
    pltpu.make_async_copy(squares_x.at[pl.ds(0, 3)], squares_x.at[pl.ds(0, 3)], sq_sem.at[0]).wait()
    pltpu.make_async_copy(squares_z.at[pl.ds(0, 7)], squares_z.at[pl.ds(0, 7)], sq_sem.at[2]).wait()
    for i in (0, 2):
        pltpu.make_async_copy(
            (got if i == 0 else got_bc).at[some if i == 0 else some_bc],
            (got if i == 0 else got_bc).at[some if i == 0 else some_bc],
            sum_sem.at[i],
        ).wait()
    for i in range(4):
        ref, span = (step_out, some) if i < 2 else (bc_out, some_bc)
        pltpu.make_async_copy(ref.at[span], ref.at[span], out_sem.at[i]).wait()


def front(hidden, norm_gain, in_weight, conv_weight, conv_bias, x_proj_weight, conv_state):
    weight = in_weight.reshape(D, 2, 2, 128).transpose(0, 2, 1, 3).reshape(4 * D, 128)
    vmem = pl.BlockSpec(memory_space=pltpu.VMEM)
    return pl.pallas_call(
        gather_kernel,
        out_shape=(
            jax.ShapeDtypeStruct((REQ, LOC), BF16),
            jax.ShapeDtypeStruct((REQ, LOC), BF16),
            jax.ShapeDtypeStruct((3, REQ, LOC), BF16),
            jax.ShapeDtypeStruct((DT_RANK, REQ), BF16),
            jax.ShapeDtypeStruct((2 * N, 1, REQ), F32),
        ),
        in_specs=[vmem, vmem, pl.BlockSpec(memory_space=pl.ANY), vmem, vmem, vmem, vmem],
        out_specs=(vmem,) * 5,
        scratch_shapes=[
            pltpu.VMEM((4 * D, 128), BF16),
            pltpu.VMEM((1024, 128), F32),
            pltpu.VMEM((D, 2 * LOC), BF16),
            pltpu.VMEM((2, DEVS, REQ, 128), BF16),
            pltpu.VMEM((REQ, 2 * LOC), F32),
            pltpu.VMEM((XS, 1, REQ), F32),
            pltpu.VMEM((ZS, 1, REQ), F32),
            pltpu.VMEM((DT_RANK, REQ), BF16),
            pltpu.VMEM((2 * N, 1, REQ), F32),
            pltpu.VMEM((DT_RANK, REQ), BF16),
            pltpu.VMEM((DEVS, 1, REQ), F32),
            pltpu.SemaphoreType.DMA((8,)),
            pltpu.SemaphoreType.DMA((2, ZS, XS)),
            pltpu.SemaphoreType.DMA((2,)),
            pltpu.SemaphoreType.DMA((4,)),
            pltpu.SemaphoreType.DMA((4,)),
            pltpu.SemaphoreType.DMA((4,)),
        ],
        compiler_params=pltpu.CompilerParams(
            collective_id=0, has_side_effects=True, vmem_limit_bytes=50 * 2**20
        ),
    )(
        hidden,
        norm_gain.reshape(1, LOC),
        weight,
        conv_weight,
        conv_bias.reshape(1, LOC),
        x_proj_weight.T,
        conv_state.transpose(1, 0, 2),
    )


def rms_scale(values, epsilon, axis):
    return values * lax.rsqrt(jnp.mean(values * values, axis=axis, keepdims=True) + epsilon)


def local(
    hidden,
    norm_gain,
    in_weight,
    conv_weight,
    conv_bias,
    x_proj_weight,
    dt_norm_gain,
    b_norm_gain,
    c_norm_gain,
    dt_weight,
    dt_bias,
    decay_log,
    skip_gain,
    conv_state,
    ssm_state,
):
    conv_act, gate_half, next_conv, step_raw, bc_raw = front(
        hidden, norm_gain, in_weight, conv_weight, conv_bias, x_proj_weight, conv_state
    )
    bc_raw = bc_raw.reshape(2 * N, REQ)
    step_normed = (
        rms_scale(step_raw.astype(F32), 1e-06, 0) * dt_norm_gain[:, None]
    ).astype(BF16)
    b_values = (rms_scale(bc_raw[:N], 1e-06, 0) * b_norm_gain[:, None]).T
    c_values = (rms_scale(bc_raw[N:], 1e-06, 0) * c_norm_gain[:, None]).T
    step_size = jax.nn.softplus(
        jnp.dot(step_normed.T, dt_weight, preferred_element_type=F32) + dt_bias
    )
    decay_rates = jnp.exp(decay_log)
    decay_factor = jnp.exp(-step_size[:, None, :] * decay_rates[None])
    act_wide = conv_act.astype(F32)
    new_state = (
        decay_factor * ssm_state.astype(F32)
        + (step_size * act_wide)[:, None, :] * b_values[:, :, None]
    )
    mixed_out = jnp.sum(new_state * c_values[:, :, None], axis=1) + skip_gain * act_wide
    output = (mixed_out * jax.nn.silu(gate_half.astype(F32))).astype(BF16)
    return (output, next_conv.transpose(1, 0, 2), new_state.astype(BF16))


def solution(mesh):
    return jax.shard_map(
        local,
        mesh=mesh,
        in_specs=(
            P("req", "chan"),
            P("chan"),
            P(None, None, "chan"),
            P(None, "chan"),
            P("chan"),
            P("chan", None),
            P(),
            P(),
            P(),
            P(None, "chan"),
            P("chan"),
            P(None, "chan"),
            P("chan"),
            P("req", None, "chan"),
            P("req", None, "chan"),
        ),
        out_specs=(P("req", "chan"), P("req", None, "chan"), P("req", None, "chan")),
        check_vma=False,
    )
```

```python
import jax
import jax.numpy as jnp
from jax import lax
from jax.experimental import pallas as pl
from jax.experimental.pallas import tpu as pltpu
from jax.sharding import PartitionSpec as P

D = 8192
N = 16
DT_RANK = 512
ZS = 8
XS = 4
DEVS = 32
REQ = 128
LOC = 256
MESH = pl.DeviceIdType.MESH
F32 = jnp.float32
BF16 = jnp.bfloat16

OWN = [
    (0, 0, 1), (0, 0, -1), (0, 1, 0), (0, -1, 0), (0, 0, 2),
    (1, 1, 0), (1, -1, 0), (1, 0, 1), (1, 0, -1), (1, 2, 0), (1, -2, 0), (1, 0, 2),
]


def passes():
    along_x = [(0, 1), (0, -1), (0, 2)]
    up, down = [(1, 0)], [(-1, 0)]
    order = [
        ((0, 0, -1), up + down), ((0, 0, 1), up + down), ((0, -1, 0), up), ((0, 1, 0), down),
        ((1, -1, 0), along_x), ((1, 1, 0), along_x), ((1, 0, -1), []), ((1, 0, 1), []),
        ((0, 0, 2), up + down),
        ((1, -2, 0), [(1, 0), (2, 0)] + along_x), ((1, 2, 0), [(-1, 0)] + along_x), ((1, 0, 2), []),
        ((0, -1, -1), up), ((0, 1, -1), down), ((0, -1, 1), up), ((0, 1, 1), down),
        ((1, -1, -1), []), ((1, -1, 1), []),
        ((0, -2, 0), [(1, 0), (2, 0)]), ((0, 2, 0), down),
        ((1, 1, -1), []), ((1, 1, 1), []),
        ((0, -1, 2), up), ((0, 1, 2), down),
        ((1, -3, 0), along_x), ((1, 3, 0), along_x),
        ((1, -1, 2), []), ((1, -2, -1), []), ((1, -2, 1), []),
        ((0, 2, -1), down), ((0, -2, -1), [(1, 0), (2, 0)]), ((1, 2, -1), []), ((0, 2, 1), [(-1, 0), (-2, 0)]),
        ((1, 2, 1), []),
        ((1, 4, 0), along_x), ((0, 3, 0), []), ((1, 1, 2), []), ((0, -2, 1), up), ((1, -2, 2), []),
        ((0, 2, 2), [(-1, 0), (-2, 0)]), ((1, 2, 2), []), ((0, -3, 0), []),
        ((1, -3, -1), []), ((1, -3, 1), []), ((0, 3, -1), []), ((1, 3, -1), []), ((1, 3, 1), []),
        ((0, -2, 2), up), ((0, 3, 1), []), ((0, 4, 0), []), ((1, -3, 2), []), ((1, 4, -1), []), ((1, 4, 1), []),
        ((0, -3, -1), []), ((0, 4, 1), []), ((1, 3, 2), []), ((0, 3, 2), []), ((1, 4, 2), []),
        ((0, -3, 1), []), ((0, 4, -1), []), ((0, 4, 2), []), ((0, -3, 2), []),
    ]
    return order


def gather_kernel(
    hidden_hbm, gain_hbm, weight_hbm, conv_weight_hbm, conv_bias_hbm, proj_hbm, conv_state_hbm,
    act_out, mixed_out, step_out, bc_out,
    hidden, gain, conv_weight, conv_bias, proj, conv_state, raw, wide, ready, units, total, squares_x, squares_z, part, part_bc, got, got_bc,
    in_sem, weight_sem, recv_sem, send_sem, sq_sem, sum_sem, out_sem,
):
    req = lax.axis_index("req")
    me = lax.axis_index("chan")
    mz = me // XS
    mx = lax.rem(me, XS)

    def place(dz, dx):
        return lax.rem(mz + dz + ZS, ZS) * XS + lax.rem(mx + dx + XS, XS)

    small_copies = [
        pltpu.make_async_copy(source, target, in_sem.at[i])
        for i, (source, target) in enumerate(
            (
                (hidden_hbm, hidden),
                (gain_hbm, gain),
                (conv_weight_hbm, conv_weight),
                (conv_bias_hbm, conv_bias),
                (proj_hbm, proj),
                (conv_state_hbm, conv_state),
            )
        )
    ]
    small_copies[0].start()
    small_copies[1].start()
    weight_copies = [
        pltpu.make_async_copy(
            weight_hbm.at[pl.ds(i * 4096, 4096)], raw.at[pl.ds(i * 4096, 4096)], weight_sem.at[i]
        )
        for i in range(8)
    ]
    greeted = [(1, 0), (-1, 0), (2, 0), (-2, 0), (0, 1), (0, -1), (0, 2)]
    barrier = pltpu.get_barrier_semaphore()
    for dz, dx in greeted:
        pl.semaphore_signal(barrier, inc=1, device_id=(req, place(dz, dx)), device_id_type=MESH)

    for copy in weight_copies:
        copy.start()
    for copy in small_copies[2:]:
        copy.start()
    small_copies[0].wait()
    small_copies[1].wait()
    widened = hidden[...].astype(F32)
    gain_rows = gain[...].astype(F32)
    for half in range(2):
        scaled = widened[:, half * 128 : half * 128 + 128] * gain_rows[half : half + 1]
        units[half, pl.ds(me, 1)] = scaled.astype(BF16)[None]
    square_row = lax.dot_general(
        jnp.ones((8, LOC), F32), widened * widened, (((1,), (1,)), ((), ())),
        precision=lax.Precision.HIGHEST, preferred_element_type=F32,
    )
    squares_x[pl.ds(mx, 1)] = square_row[None, :1]

    pl.semaphore_wait(barrier, len(greeted))

    def push(half, dz, dx, hz, hx):
        owner = place(dz, dx)
        pltpu.make_async_remote_copy(
            units.at[half, owner], units.at[half, owner], send_sem.at[half],
            recv_sem.at[half, (dz - hz) % ZS, (dx - hx) % XS],
            device_id=(req, place(hz, hx)), device_id_type=MESH,
        ).start()

    def await_unit(half, dz, dx):
        owner = place(dz, dx)
        pltpu.make_async_copy(
            units.at[half, owner], units.at[half, owner], recv_sem.at[half, dz % ZS, dx % XS]
        ).wait()

    for half, hz, hx in OWN:
        push(half, 0, 0, hz, hx)
    for dx in (1, -1, 2):
        pltpu.make_async_remote_copy(
            squares_x.at[mx], squares_x.at[mx], sq_sem.at[0], sq_sem.at[1],
            device_id=(req, place(0, dx)), device_id_type=MESH,
        ).start()

    def convert(index, _):
        wide[...] = raw[pl.ds(pl.multiple_of(index * 1024, 1024), 1024), :].astype(F32)
        for side in range(2):
            for tile in range(2):
                column = side * 256 + tile * 128
                ready[pl.ds(pl.multiple_of(index * 256, 256), 256), column : column + 128] = wide[
                    pl.ds(2 * tile + side, 256, stride=4), :
                ].astype(BF16)
        return 0

    def multiply(dz, dx, first=False):
        owner = place(dz, dx)
        left = jnp.concatenate([units[0, owner], units[1, owner]], axis=1)
        product = jnp.dot(
            left, ready[pl.ds(pl.multiple_of(owner * 256, 256), 256), :], preferred_element_type=F32
        )
        total[...] = product if first else total[...] + product

    converted = 0

    def convert_to(count):
        nonlocal converted
        while converted < count:
            if converted % 4 == 0:
                weight_copies[converted // 4].wait()
            last = min(count, converted // 4 * 4 + 4)
            lax.fori_loop(converted, last, convert, 0)
            converted = last

    convert_to(8)
    arrived = {}
    pending = []
    started = False
    column = 0
    order = passes()
    for step, ((half, dz, dx), hops) in enumerate(order):
        await_unit(half, dz, dx)
        for hz, hx in hops:
            push(half, dz, dx, hz, hx)
        arrived[(dz, dx)] = arrived.get((dz, dx), 0) + 1
        if arrived[(dz, dx)] == 2:
            pending.append((dz, dx))
        if dx == 0 and half == 1:
            column += 1
            if column == 7:
                pltpu.make_async_copy(
                    squares_x.at[pl.ds(0, 3)], squares_x.at[pl.ds(0, 3)], sq_sem.at[1]
                ).wait()
                squares_z[pl.ds(mz, 1)] = jnp.sum(squares_x[...], axis=0, keepdims=True)
                for hz in (1, -1, 2, -2, 3, -3, 4):
                    pltpu.make_async_remote_copy(
                        squares_z.at[mz], squares_z.at[mz], sq_sem.at[2], sq_sem.at[3],
                        device_id=(req, place(hz, 0)), device_id_type=MESH,
                    ).start()
        if converted < DEVS:
            convert_to(min(DEVS, converted + 2))
        elif pending:
            if not started:
                multiply(0, 0, True)
                started = True
            multiply(*pending.pop(0))
    while pending:
        multiply(*pending.pop(0))

    pltpu.make_async_copy(squares_z.at[pl.ds(0, 7)], squares_z.at[pl.ds(0, 7)], sq_sem.at[3]).wait()
    row = jnp.sum(squares_z[...], axis=0)
    inverse_row = lax.rsqrt(row / D + 1e-05)
    inverse = jnp.transpose(jnp.broadcast_to(inverse_row, (128, 128)))
    for copy in small_copies[2:]:
        copy.wait()
    mixed = [
        (total[:, i * 128 : i * 128 + 128] * inverse).astype(BF16) for i in range(4)
    ]
    new_inputs = jnp.concatenate(mixed[:2], axis=1)
    mixed_out[...] = jnp.concatenate(mixed, axis=1)
    window = conv_state[0].astype(F32) * conv_weight[0:1]
    window += conv_state[1].astype(F32) * conv_weight[1:2]
    window += conv_state[2].astype(F32) * conv_weight[2:3]
    window += new_inputs.astype(F32) * conv_weight[3:4]
    window += conv_bias[...]
    act = (window * jax.nn.sigmoid(window)).astype(BF16)
    act_out[...] = act
    projected = lax.dot_general(
        proj[...], act, (((1,), (1,)), ((), ())), preferred_element_type=F32
    )
    part[...] = projected[:DT_RANK].astype(BF16)
    for i in range(2 * N):
        part_bc[i] = projected[DT_RANK + i : DT_RANK + i + 1]

    def rows(index):
        return pl.ds(pl.multiple_of(index * 16, 16), 16)

    def spread(i, _):
        peer = lax.rem(me + i, DEVS)
        pltpu.make_async_remote_copy(
            part.at[rows(peer)], got.at[rows(me)], sum_sem.at[0], sum_sem.at[1],
            device_id=(req, peer), device_id_type=MESH,
        ).start()
        pltpu.make_async_remote_copy(
            part_bc.at[peer], got_bc.at[me], sum_sem.at[2], sum_sem.at[3],
            device_id=(req, peer), device_id_type=MESH,
        ).start()
        return 0

    lax.fori_loop(1, DEVS, spread, 0)
    got[rows(me), :] = part[rows(me), :]
    got_bc[pl.ds(me, 1)] = part_bc[pl.ds(me, 1)]

    some, some_bc = pl.ds(0, 31 * 16), pl.ds(0, 31)
    pltpu.make_async_copy(got.at[some], got.at[some], sum_sem.at[1]).wait()
    pltpu.make_async_copy(got_bc.at[some_bc], got_bc.at[some_bc], sum_sem.at[3]).wait()
    step = got[0:16].astype(F32)
    for i in range(1, DEVS):
        step += got[i * 16 : i * 16 + 16].astype(F32)
    step_out[rows(me), :] = step.astype(BF16)
    bc_out[pl.ds(me, 1)] = jnp.sum(got_bc[...], axis=0, keepdims=True)

    def share(i, _):
        peer = lax.rem(me + i, DEVS)
        pltpu.make_async_remote_copy(
            step_out.at[rows(me)], step_out.at[rows(me)], out_sem.at[0], out_sem.at[1],
            device_id=(req, peer), device_id_type=MESH,
        ).start()
        pltpu.make_async_remote_copy(
            bc_out.at[me], bc_out.at[me], out_sem.at[2], out_sem.at[3],
            device_id=(req, peer), device_id_type=MESH,
        ).start()
        return 0

    lax.fori_loop(1, DEVS, share, 0)
    for half in range(2):
        pltpu.make_async_copy(
            units.at[half, pl.ds(0, 31)], units.at[half, pl.ds(0, 31)], send_sem.at[half]
        ).wait()
    pltpu.make_async_copy(squares_x.at[pl.ds(0, 3)], squares_x.at[pl.ds(0, 3)], sq_sem.at[0]).wait()
    pltpu.make_async_copy(squares_z.at[pl.ds(0, 7)], squares_z.at[pl.ds(0, 7)], sq_sem.at[2]).wait()
    for i in (0, 2):
        pltpu.make_async_copy(
            (got if i == 0 else got_bc).at[some if i == 0 else some_bc],
            (got if i == 0 else got_bc).at[some if i == 0 else some_bc],
            sum_sem.at[i],
        ).wait()
    for i in range(4):
        ref, span = (step_out, some) if i < 2 else (bc_out, some_bc)
        pltpu.make_async_copy(ref.at[span], ref.at[span], out_sem.at[i]).wait()


def front(hidden, norm_gain, in_weight, conv_weight, conv_bias, x_proj_weight, conv_state):
    weight = in_weight.reshape(D, 2, 2, 128).transpose(0, 2, 1, 3).reshape(4 * D, 128)
    vmem = pl.BlockSpec(memory_space=pltpu.VMEM)
    return pl.pallas_call(
        gather_kernel,
        out_shape=(
            pltpu.VMEM((REQ, LOC), BF16),
            pltpu.VMEM((REQ, 2 * LOC), BF16),
            pltpu.VMEM((DT_RANK, REQ), BF16),
            pltpu.VMEM((2 * N, 1, REQ), F32),
        ),
        in_specs=[pl.BlockSpec(memory_space=pltpu.HBM)] * 7,
        out_specs=(vmem,) * 4,
        scratch_shapes=[
            pltpu.VMEM((REQ, LOC), BF16),
            pltpu.VMEM((2, 128), BF16),
            pltpu.VMEM((4, LOC), F32),
            pltpu.VMEM((1, LOC), F32),
            pltpu.VMEM((DT_RANK + 2 * N, LOC), BF16),
            pltpu.VMEM((3, REQ, LOC), BF16),
            pltpu.VMEM((4 * D, 128), BF16),
            pltpu.VMEM((1024, 128), F32),
            pltpu.VMEM((D, 2 * LOC), BF16),
            pltpu.VMEM((2, DEVS, REQ, 128), BF16),
            pltpu.VMEM((REQ, 2 * LOC), F32),
            pltpu.VMEM((XS, 1, REQ), F32),
            pltpu.VMEM((ZS, 1, REQ), F32),
            pltpu.VMEM((DT_RANK, REQ), BF16),
            pltpu.VMEM((2 * N, 1, REQ), F32),
            pltpu.VMEM((DT_RANK, REQ), BF16),
            pltpu.VMEM((DEVS, 1, REQ), F32),
            pltpu.SemaphoreType.DMA((6,)),
            pltpu.SemaphoreType.DMA((8,)),
            pltpu.SemaphoreType.DMA((2, ZS, XS)),
            pltpu.SemaphoreType.DMA((2,)),
            pltpu.SemaphoreType.DMA((4,)),
            pltpu.SemaphoreType.DMA((4,)),
            pltpu.SemaphoreType.DMA((4,)),
        ],
        compiler_params=pltpu.CompilerParams(
            collective_id=0, has_side_effects=True, vmem_limit_bytes=56 * 2**20
        ),
    )(
        hidden,
        norm_gain.reshape(2, 128),
        weight,
        conv_weight,
        conv_bias.reshape(1, LOC),
        x_proj_weight.T,
        conv_state.transpose(1, 0, 2),
    )


BLOCKS = 4
ROWS = REQ // BLOCKS


def state_kernel(
    act, mixed, step_raw, bc_raw, dt_gain, b_gain, c_gain, dt_weight, dt_bias, decay_log, skip_gain, conv_state, state,
    out, next_conv, next_state,
    step_size, drive, b_turned, c_turned,
):
    block = pl.program_id(0)

    @pl.when(block == 0)
    def _():
        raw = step_raw[...].astype(F32)
        scale = lax.rsqrt(jnp.mean(raw * raw, axis=0, keepdims=True) + 1e-06)
        normed = (jnp.transpose(raw * scale) * dt_gain[...]).astype(BF16)
        before = jnp.dot(normed, dt_weight[...], preferred_element_type=F32) + dt_bias[...]
        size = jnp.maximum(before, 0.0) + jnp.log1p(jnp.exp(-jnp.abs(before)))
        step_size[...] = size
        drive[...] = size * act[...].astype(F32)
        square = (N, N)
        eye = lax.broadcasted_iota(jnp.int32, square, 0) == lax.broadcasted_iota(jnp.int32, square, 1)
        for part, gain_row, turned in ((0, b_gain, b_turned), (N, c_gain, c_turned)):
            column = jnp.sum(
                jnp.where(eye, jnp.broadcast_to(gain_row[...], square), 0.0), axis=1, keepdims=True
            )
            values = bc_raw[part : part + N]
            scale = lax.rsqrt(jnp.mean(values * values, axis=0, keepdims=True) + 1e-06)
            values = values * scale * column
            for i in range(BLOCKS):
                turned[i] = pltpu.roll(values, REQ - i * ROWS, 1) if i else values

    rows = pl.ds(pl.multiple_of(block * ROWS, ROWS), ROWS)
    rates = -jnp.exp(decay_log[...])
    b_here = b_turned[block]
    c_here = c_turned[block]
    sums = []
    for r in range(ROWS):
        row = pl.ds(block * ROWS + r, 1)
        decay = jnp.exp(step_size[row, :] * rates)
        new = decay * state[r].astype(F32) + drive[row, :] * b_here[:, r : r + 1]
        next_state[r] = new.astype(BF16)
        sums.append(jnp.sum(new * c_here[:, r : r + 1], axis=0, keepdims=True))
    summed = jnp.concatenate(sums, axis=0)
    act_wide = act[rows, :].astype(F32)
    gate = mixed[rows, LOC:].astype(F32)
    out[...] = ((summed + skip_gain[...] * act_wide) * (gate * jax.nn.sigmoid(gate))).astype(BF16)
    next_conv[0:2] = conv_state[1:3, rows, :]
    next_conv[2] = mixed[rows, :LOC]


def local(
    hidden,
    norm_gain,
    in_weight,
    conv_weight,
    conv_bias,
    x_proj_weight,
    dt_norm_gain,
    b_norm_gain,
    c_norm_gain,
    dt_weight,
    dt_bias,
    decay_log,
    skip_gain,
    conv_state,
    ssm_state,
):
    act, mixed, step_raw, bc_raw = front(
        hidden, norm_gain, in_weight, conv_weight, conv_bias, x_proj_weight, conv_state
    )
    whole = pl.BlockSpec(memory_space=pltpu.VMEM)
    output, next_conv, next_state = pl.pallas_call(
        state_kernel,
        grid=(BLOCKS,),
        out_shape=(
            jax.ShapeDtypeStruct((REQ, LOC), BF16),
            jax.ShapeDtypeStruct((3, REQ, LOC), BF16),
            jax.ShapeDtypeStruct((REQ, N, LOC), BF16),
        ),
        in_specs=[whole] * 12 + [pl.BlockSpec((ROWS, N, LOC), lambda i: (i, 0, 0))],
        out_specs=(
            pl.BlockSpec((ROWS, LOC), lambda i: (i, 0)),
            pl.BlockSpec((3, ROWS, LOC), lambda i: (0, i, 0)),
            pl.BlockSpec((ROWS, N, LOC), lambda i: (i, 0, 0)),
        ),
        scratch_shapes=[
            pltpu.VMEM((REQ, LOC), F32),
            pltpu.VMEM((REQ, LOC), F32),
            pltpu.VMEM((BLOCKS, N, REQ), F32),
            pltpu.VMEM((BLOCKS, N, REQ), F32),
        ],
        compiler_params=pltpu.CompilerParams(vmem_limit_bytes=24 * 2**20),
    )(
        act,
        mixed,
        step_raw,
        bc_raw.reshape(2 * N, REQ),
        dt_norm_gain.reshape(1, DT_RANK),
        b_norm_gain.reshape(1, N),
        c_norm_gain.reshape(1, N),
        dt_weight,
        dt_bias.reshape(1, LOC),
        decay_log,
        skip_gain.reshape(1, LOC),
        conv_state.transpose(1, 0, 2),
        ssm_state,
    )
    return (output, next_conv.transpose(1, 0, 2), next_state)


def solution(mesh):
    return jax.shard_map(
        local,
        mesh=mesh,
        in_specs=(
            P("req", "chan"),
            P("chan"),
            P(None, None, "chan"),
            P(None, "chan"),
            P("chan"),
            P("chan", None),
            P(),
            P(),
            P(),
            P(None, "chan"),
            P("chan"),
            P(None, "chan"),
            P("chan"),
            P("req", None, "chan"),
            P("req", None, "chan"),
        ),
        out_specs=(P("req", "chan"), P("req", None, "chan"), P("req", None, "chan")),
        check_vma=False,
    )
```

```python
import jax
import jax.numpy as jnp
from jax import lax
from jax.experimental import pallas as pl
from jax.experimental.pallas import tpu as pltpu
from jax.sharding import PartitionSpec as P

D = 8192
N = 16
DT_RANK = 512
ZS = 8
XS = 4
DEVS = 32
REQ = 128
LOC = 256
MESH = pl.DeviceIdType.MESH
F32 = jnp.float32
BF16 = jnp.bfloat16

GREETED = ((-2, 0), (0, 2), (2, 0), (-1, 0), (0, -1), (0, 1), (1, 0))
OWN = (
    (1, -1, 0), (0, 2, 0), (1, 0, -1), (1, 0, 1), (0, 0, -1), (0, 0, 1), (0, -2, 0), (0, 0, 2), (1, -2, 0),
    (1, 0, 2), (1, 1, 0), (0, 1, 0), (1, 2, 0),
)
PASSES = (
    ((1, -1, 0), ((-2, 0), (0, -1), (0, 1))), ((1, 0, -1), ((1, 0), )), ((1, 0, 1), ()),
    ((0, 2, 0), ((0, 2), (1, 0), (0, -1), (0, 1))), ((0, 0, -1), ((1, 0), )), ((0, 0, 1), ((-1, 0), )),
    ((1, 1, 0), ((0, 1), )), ((0, -2, 0), ((-1, 0), (0, -1), (-2, 0), (0, 2))), ((0, 1, 0), ((0, 1), )),
    ((0, 0, 2), ()), ((1, 0, 2), ((2, 0), )), ((1, -2, 0), ((0, -1), )), ((1, 2, 0), ((1, 0), )),
    ((1, -1, -1), ((0, -1), )), ((1, -1, 1), ((-1, 0), )), ((1, 1, -1), ((1, 0), )),
    ((1, -3, 0), ((0, 1), (0, -1), (-1, 0))), ((0, 2, -1), ()), ((0, 2, 1), ()), ((0, 3, 0), ((0, 1), (0, -1))),
    ((0, -1, 1), ((0, 1), (-1, 0), (0, -1))), ((0, 2, 2), ((1, 0), (-1, 0))), ((0, 1, -1), ()),
    ((0, -3, 0), ((0, 1), )), ((0, -2, -1), ((-1, 0), (1, 0))), ((1, 1, 1), ((0, 1), (1, 0))),
    ((1, -2, -1), ((0, -1), )), ((0, 1, 1), ()), ((1, 2, 2), ((1, 0), )), ((0, 4, 0), ((0, 1), (0, -1))),
    ((0, -2, 2), ((-1, 0), )), ((1, 3, 0), ((0, 1), )), ((1, -2, 1), ()), ((1, -1, 2), ()),
    ((1, -3, 1), ((0, 1), (-1, 0))), ((1, 2, -1), ((1, 0), )), ((1, 4, 0), ((0, 2), )), ((1, -3, -1), ((-1, 0), )),
    ((0, 3, 1), ()), ((0, 3, 2), ((1, 0), )), ((0, -2, 1), ()), ((0, 3, -1), ()), ((0, -1, 2), ()),
    ((0, -1, -1), ()), ((0, 1, 2), ()), ((0, -1, 0), ()), ((0, -3, 1), ()), ((1, 2, 1), ()), ((0, -3, -1), ()),
    ((1, -2, 2), ()), ((1, 1, 2), ()), ((1, 3, 2), ()), ((0, -3, 2), ()), ((0, 4, -1), ()), ((0, 4, 1), ()),
    ((1, 4, 1), ()), ((1, 3, -1), ()), ((1, 3, 1), ()), ((1, 4, -1), ()), ((0, 4, 2), ()), ((1, 4, 2), ()),
    ((1, -3, 2), ()),
)


def gather_kernel(
    hidden_hbm, gain_hbm, weight_hbm, conv_weight_hbm, conv_bias_hbm, proj_hbm, conv_state_hbm,
    act_out, mixed_out, step_out, bc_out,
    hidden, gain, conv_weight, conv_bias, proj, conv_state, raw, wide, ready, units, total, squares_x, squares_z, part, part_bc, got, got_bc,
    in_sem, weight_sem, recv_sem, send_sem, sq_sem, sum_sem, out_sem,
):
    req = lax.axis_index("req")
    me = lax.axis_index("chan")
    mz = me // XS
    mx = lax.rem(me, XS)

    def place(dz, dx):
        return lax.rem(mz + dz + ZS, ZS) * XS + lax.rem(mx + dx + XS, XS)

    small_copies = [
        pltpu.make_async_copy(source, target, in_sem.at[i])
        for i, (source, target) in enumerate(
            (
                (hidden_hbm, hidden),
                (gain_hbm, gain),
                (conv_weight_hbm, conv_weight),
                (conv_bias_hbm, conv_bias),
                (proj_hbm, proj),
                (conv_state_hbm, conv_state),
            )
        )
    ]
    small_copies[0].start()
    small_copies[1].start()
    weight_copies = [
        pltpu.make_async_copy(
            weight_hbm.at[pl.ds(i * 4096, 4096)], raw.at[pl.ds(i * 4096, 4096)], weight_sem.at[i]
        )
        for i in range(8)
    ]
    barrier = pltpu.get_barrier_semaphore()
    for hz, hx in GREETED:
        pl.semaphore_signal(barrier, inc=1, device_id=(req, place(-hz, -hx)), device_id_type=MESH)

    for copy in weight_copies:
        copy.start()
    for copy in small_copies[2:]:
        copy.start()
    small_copies[0].wait()
    small_copies[1].wait()
    widened = hidden[...].astype(F32)
    gain_rows = gain[...].astype(F32)
    for half in range(2):
        scaled = widened[:, half * 128 : half * 128 + 128] * gain_rows[half : half + 1]
        units[half, pl.ds(me, 1)] = scaled.astype(BF16)[None]
    square_row = lax.dot_general(
        jnp.ones((8, LOC), F32), widened * widened, (((1,), (1,)), ((), ())),
        precision=lax.Precision.HIGHEST, preferred_element_type=F32,
    )
    squares_x[pl.ds(mx, 1)] = square_row[None, :1]

    pl.semaphore_wait(barrier, len(GREETED))

    def push(half, z, x, hz, hx):
        owner = place(-z, -x)
        pltpu.make_async_remote_copy(
            units.at[half, owner], units.at[half, owner], send_sem.at[half],
            recv_sem.at[half, (z + hz) % ZS, (x + hx) % XS],
            device_id=(req, place(hz, hx)), device_id_type=MESH,
        ).start()

    def await_unit(half, z, x):
        owner = place(-z, -x)
        pltpu.make_async_copy(
            units.at[half, owner], units.at[half, owner], recv_sem.at[half, z % ZS, x % XS]
        ).wait()

    for half, hz, hx in OWN:
        push(half, 0, 0, hz, hx)
    for dx in (1, -1, 2):
        pltpu.make_async_remote_copy(
            squares_x.at[mx], squares_x.at[mx], sq_sem.at[0], sq_sem.at[1],
            device_id=(req, place(0, dx)), device_id_type=MESH,
        ).start()

    def convert(index, _):
        wide[...] = raw[pl.ds(pl.multiple_of(index * 1024, 1024), 1024), :].astype(F32)
        for side in range(2):
            for tile in range(2):
                column = side * 256 + tile * 128
                ready[pl.ds(pl.multiple_of(index * 256, 256), 256), column : column + 128] = wide[
                    pl.ds(2 * tile + side, 256, stride=4), :
                ].astype(BF16)
        return 0

    def multiply(z, x, first=False):
        owner = place(-z, -x)
        left = jnp.concatenate([units[0, owner], units[1, owner]], axis=1)
        product = jnp.dot(
            left, ready[pl.ds(pl.multiple_of(owner * 256, 256), 256), :], preferred_element_type=F32
        )
        total[...] = product if first else total[...] + product

    converted = 0

    def convert_to(count):
        nonlocal converted
        while converted < count:
            if converted % 4 == 0:
                weight_copies[converted // 4].wait()
            last = min(count, converted // 4 * 4 + 4)
            lax.fori_loop(converted, last, convert, 0)
            converted = last

    convert_to(8)
    arrived = {}
    pending = []
    started = False
    column = {0}
    for (half, z, x), moves in PASSES:
        await_unit(half, z, x)
        for hz, hx in moves:
            push(half, z, x, hz, hx)
        arrived[(z, x)] = arrived.get((z, x), 0) + 1
        if arrived[(z, x)] == 2:
            pending.append((z, x))
        if x == 0 and z not in column:
            column.add(z)
            if len(column) == ZS:
                pltpu.make_async_copy(
                    squares_x.at[pl.ds(0, 3)], squares_x.at[pl.ds(0, 3)], sq_sem.at[1]
                ).wait()
                squares_z[pl.ds(mz, 1)] = jnp.sum(squares_x[...], axis=0, keepdims=True)
                for hz in (1, -1, 2, -2, 3, -3, 4):
                    pltpu.make_async_remote_copy(
                        squares_z.at[mz], squares_z.at[mz], sq_sem.at[2], sq_sem.at[3],
                        device_id=(req, place(hz, 0)), device_id_type=MESH,
                    ).start()
        if converted < DEVS:
            convert_to(min(DEVS, converted + 2))
        elif pending:
            if not started:
                multiply(0, 0, True)
                started = True
            multiply(*pending.pop(0))
    while pending:
        multiply(*pending.pop(0))

    pltpu.make_async_copy(squares_z.at[pl.ds(0, 7)], squares_z.at[pl.ds(0, 7)], sq_sem.at[3]).wait()
    row = jnp.sum(squares_z[...], axis=0)
    inverse_row = lax.rsqrt(row / D + 1e-05)
    inverse = jnp.transpose(jnp.broadcast_to(inverse_row, (128, 128)))
    for copy in small_copies[2:]:
        copy.wait()
    mixed = [
        (total[:, i * 128 : i * 128 + 128] * inverse).astype(BF16) for i in range(4)
    ]
    new_inputs = jnp.concatenate(mixed[:2], axis=1)
    mixed_out[...] = jnp.concatenate(mixed, axis=1)
    window = conv_state[0].astype(F32) * conv_weight[0:1]
    window += conv_state[1].astype(F32) * conv_weight[1:2]
    window += conv_state[2].astype(F32) * conv_weight[2:3]
    window += new_inputs.astype(F32) * conv_weight[3:4]
    window += conv_bias[...]
    act = (window * jax.nn.sigmoid(window)).astype(BF16)
    act_out[...] = act
    projected = lax.dot_general(
        proj[...], act, (((1,), (1,)), ((), ())), preferred_element_type=F32
    )
    part[...] = projected[:DT_RANK].astype(BF16)
    for i in range(2 * N):
        part_bc[i] = projected[DT_RANK + i : DT_RANK + i + 1]

    def rows(index):
        return pl.ds(pl.multiple_of(index * 16, 16), 16)

    def spread(i, _):
        peer = lax.rem(me + i, DEVS)
        pltpu.make_async_remote_copy(
            part.at[rows(peer)], got.at[rows(me)], sum_sem.at[0], sum_sem.at[1],
            device_id=(req, peer), device_id_type=MESH,
        ).start()
        pltpu.make_async_remote_copy(
            part_bc.at[peer], got_bc.at[me], sum_sem.at[2], sum_sem.at[3],
            device_id=(req, peer), device_id_type=MESH,
        ).start()
        return 0

    lax.fori_loop(1, DEVS, spread, 0)
    got[rows(me), :] = part[rows(me), :]
    got_bc[pl.ds(me, 1)] = part_bc[pl.ds(me, 1)]

    some, some_bc = pl.ds(0, 31 * 16), pl.ds(0, 31)
    pltpu.make_async_copy(got.at[some], got.at[some], sum_sem.at[1]).wait()
    pltpu.make_async_copy(got_bc.at[some_bc], got_bc.at[some_bc], sum_sem.at[3]).wait()
    step = got[0:16].astype(F32)
    for i in range(1, DEVS):
        step += got[i * 16 : i * 16 + 16].astype(F32)
    step_out[rows(me), :] = step.astype(BF16)
    bc_out[pl.ds(me, 1)] = jnp.sum(got_bc[...], axis=0, keepdims=True)

    def share(i, _):
        peer = lax.rem(me + i, DEVS)
        pltpu.make_async_remote_copy(
            step_out.at[rows(me)], step_out.at[rows(me)], out_sem.at[0], out_sem.at[1],
            device_id=(req, peer), device_id_type=MESH,
        ).start()
        pltpu.make_async_remote_copy(
            bc_out.at[me], bc_out.at[me], out_sem.at[2], out_sem.at[3],
            device_id=(req, peer), device_id_type=MESH,
        ).start()
        return 0

    lax.fori_loop(1, DEVS, share, 0)
    for half in range(2):
        pltpu.make_async_copy(
            units.at[half, pl.ds(0, 31)], units.at[half, pl.ds(0, 31)], send_sem.at[half]
        ).wait()
    pltpu.make_async_copy(squares_x.at[pl.ds(0, 3)], squares_x.at[pl.ds(0, 3)], sq_sem.at[0]).wait()
    pltpu.make_async_copy(squares_z.at[pl.ds(0, 7)], squares_z.at[pl.ds(0, 7)], sq_sem.at[2]).wait()
    for i in (0, 2):
        pltpu.make_async_copy(
            (got if i == 0 else got_bc).at[some if i == 0 else some_bc],
            (got if i == 0 else got_bc).at[some if i == 0 else some_bc],
            sum_sem.at[i],
        ).wait()
    for i in range(4):
        ref, span = (step_out, some) if i < 2 else (bc_out, some_bc)
        pltpu.make_async_copy(ref.at[span], ref.at[span], out_sem.at[i]).wait()


def front(hidden, norm_gain, in_weight, conv_weight, conv_bias, x_proj_weight, conv_state):
    weight = in_weight.reshape(D, 2, 2, 128).transpose(0, 2, 1, 3).reshape(4 * D, 128)
    vmem = pl.BlockSpec(memory_space=pltpu.VMEM)
    return pl.pallas_call(
        gather_kernel,
        out_shape=(
            pltpu.VMEM((REQ, LOC), BF16),
            pltpu.VMEM((REQ, 2 * LOC), BF16),
            pltpu.VMEM((DT_RANK, REQ), BF16),
            pltpu.VMEM((2 * N, 1, REQ), F32),
        ),
        in_specs=[pl.BlockSpec(memory_space=pltpu.HBM)] * 7,
        out_specs=(vmem,) * 4,
        scratch_shapes=[
            pltpu.VMEM((REQ, LOC), BF16),
            pltpu.VMEM((2, 128), BF16),
            pltpu.VMEM((4, LOC), F32),
            pltpu.VMEM((1, LOC), F32),
            pltpu.VMEM((DT_RANK + 2 * N, LOC), BF16),
            pltpu.VMEM((3, REQ, LOC), BF16),
            pltpu.VMEM((4 * D, 128), BF16),
            pltpu.VMEM((1024, 128), F32),
            pltpu.VMEM((D, 2 * LOC), BF16),
            pltpu.VMEM((2, DEVS, REQ, 128), BF16),
            pltpu.VMEM((REQ, 2 * LOC), F32),
            pltpu.VMEM((XS, 1, REQ), F32),
            pltpu.VMEM((ZS, 1, REQ), F32),
            pltpu.VMEM((DT_RANK, REQ), BF16),
            pltpu.VMEM((2 * N, 1, REQ), F32),
            pltpu.VMEM((DT_RANK, REQ), BF16),
            pltpu.VMEM((DEVS, 1, REQ), F32),
            pltpu.SemaphoreType.DMA((6,)),
            pltpu.SemaphoreType.DMA((8,)),
            pltpu.SemaphoreType.DMA((2, ZS, XS)),
            pltpu.SemaphoreType.DMA((2,)),
            pltpu.SemaphoreType.DMA((4,)),
            pltpu.SemaphoreType.DMA((4,)),
            pltpu.SemaphoreType.DMA((4,)),
        ],
        compiler_params=pltpu.CompilerParams(
            collective_id=0, has_side_effects=True, vmem_limit_bytes=56 * 2**20
        ),
    )(
        hidden,
        norm_gain.reshape(2, 128),
        weight,
        conv_weight,
        conv_bias.reshape(1, LOC),
        x_proj_weight.T,
        conv_state.transpose(1, 0, 2),
    )


CHUNKS = 8
ROWS = REQ // CHUNKS


def state_kernel(
    act, mixed, step_raw, bc_raw, dt_gain, b_gain, c_gain, dt_weight, dt_bias, decay_log, skip_gain, conv_state, state,
    out_hbm, next_conv_hbm, next_state_hbm,
    step_size, drive, out, next_conv, next_state, sem,
):
    next_conv[0:2] = conv_state[1:3]
    next_conv[2] = mixed[:, :LOC]
    conv_copy = pltpu.make_async_copy(next_conv, next_conv_hbm, sem.at[CHUNKS])
    conv_copy.start()
    raw = step_raw[...].astype(F32)
    scale = lax.rsqrt(jnp.mean(raw * raw, axis=0, keepdims=True) + 1e-06)
    normed = (jnp.transpose(raw * scale) * dt_gain[...]).astype(BF16)
    before = jnp.dot(normed, dt_weight[...], preferred_element_type=F32) + dt_bias[...]
    size = jnp.maximum(before, 0.0) + jnp.log1p(jnp.exp(-jnp.abs(before)))
    step_size[...] = size
    drive[...] = size * act[...].astype(F32)
    square = (N, N)
    eye = lax.broadcasted_iota(jnp.int32, square, 0) == lax.broadcasted_iota(jnp.int32, square, 1)
    turned = []
    for part, gain_row in ((0, b_gain), (N, c_gain)):
        column = jnp.sum(
            jnp.where(eye, jnp.broadcast_to(gain_row[...], square), 0.0), axis=1, keepdims=True
        )
        values = bc_raw[part : part + N]
        scale = lax.rsqrt(jnp.mean(values * values, axis=0, keepdims=True) + 1e-06)
        turned.append(values * scale * column)
    b_turned, c_turned = turned
    rates = -jnp.exp(decay_log[...])
    copies = [conv_copy]
    for chunk in range(CHUNKS):
        rows = slice(chunk * ROWS, chunk * ROWS + ROWS)
        sums = []
        for r in range(chunk * ROWS, chunk * ROWS + ROWS):
            decay = jnp.exp(step_size[r : r + 1, :] * rates)
            new = decay * state[r].astype(F32) + drive[r : r + 1, :] * b_turned[:, r : r + 1]
            next_state[r] = new.astype(BF16)
            sums.append(jnp.sum(new * c_turned[:, r : r + 1], axis=0, keepdims=True))
        copies.append(
            pltpu.make_async_copy(next_state.at[rows], next_state_hbm.at[rows], sem.at[chunk])
        )
        copies[-1].start()
        summed = jnp.concatenate(sums, axis=0)
        act_wide = act[rows, :].astype(F32)
        gate = mixed[rows, LOC:].astype(F32)
        gated = (summed + skip_gain[...] * act_wide) * (gate * jax.nn.sigmoid(gate))
        out[rows, :] = gated.astype(BF16)
    copies.append(pltpu.make_async_copy(out, out_hbm, sem.at[CHUNKS + 1]))
    copies[-1].start()
    for copy in copies:
        copy.wait()


def local(
    hidden,
    norm_gain,
    in_weight,
    conv_weight,
    conv_bias,
    x_proj_weight,
    dt_norm_gain,
    b_norm_gain,
    c_norm_gain,
    dt_weight,
    dt_bias,
    decay_log,
    skip_gain,
    conv_state,
    ssm_state,
):
    act, mixed, step_raw, bc_raw = front(
        hidden, norm_gain, in_weight, conv_weight, conv_bias, x_proj_weight, conv_state
    )
    whole = pl.BlockSpec(memory_space=pltpu.VMEM)
    output, next_conv, next_state = pl.pallas_call(
        state_kernel,
        out_shape=(
            jax.ShapeDtypeStruct((REQ, LOC), BF16),
            jax.ShapeDtypeStruct((3, REQ, LOC), BF16),
            jax.ShapeDtypeStruct((REQ, N, LOC), BF16),
        ),
        in_specs=[whole] * 13,
        out_specs=(pl.BlockSpec(memory_space=pl.ANY),) * 3,
        scratch_shapes=[
            pltpu.VMEM((REQ, LOC), F32),
            pltpu.VMEM((REQ, LOC), F32),
            pltpu.VMEM((REQ, LOC), BF16),
            pltpu.VMEM((3, REQ, LOC), BF16),
            pltpu.VMEM((REQ, N, LOC), BF16),
            pltpu.SemaphoreType.DMA((CHUNKS + 2,)),
        ],
        compiler_params=pltpu.CompilerParams(vmem_limit_bytes=24 * 2**20),
    )(
        act,
        mixed,
        step_raw,
        bc_raw.reshape(2 * N, REQ),
        dt_norm_gain.reshape(1, DT_RANK),
        b_norm_gain.reshape(1, N),
        c_norm_gain.reshape(1, N),
        dt_weight,
        dt_bias.reshape(1, LOC),
        decay_log,
        skip_gain.reshape(1, LOC),
        conv_state.transpose(1, 0, 2),
        ssm_state,
    )
    return (output, next_conv.transpose(1, 0, 2), next_state)


def solution(mesh):
    return jax.shard_map(
        local,
        mesh=mesh,
        in_specs=(
            P("req", "chan"),
            P("chan"),
            P(None, None, "chan"),
            P(None, "chan"),
            P("chan"),
            P("chan", None),
            P(),
            P(),
            P(),
            P(None, "chan"),
            P("chan"),
            P(None, "chan"),
            P("chan"),
            P("req", None, "chan"),
            P("req", None, "chan"),
        ),
        out_specs=(P("req", "chan"), P("req", None, "chan"), P("req", None, "chan")),
        check_vma=False,
    )
```

```python
import jax
import jax.numpy as jnp
from jax import lax
from jax.experimental import pallas as pl
from jax.experimental.pallas import tpu as pltpu
from jax.sharding import PartitionSpec as P

D = 8192
N = 16
DT_RANK = 512
ZS = 8
XS = 4
DEVS = 32
REQ = 128
LOC = 256
MESH = pl.DeviceIdType.MESH
F32 = jnp.float32
BF16 = jnp.bfloat16

GREETED = ((-2, 0), (0, 2), (2, 0), (-1, 0), (0, -1), (0, 1), (1, 0))
OWN = (
    (1, -1, 0), (0, 2, 0), (1, 0, -1), (1, 0, 1), (0, 0, -1), (0, 0, 1), (0, -2, 0), (0, 0, 2), (1, -2, 0),
    (1, 0, 2), (1, 1, 0), (0, 1, 0), (1, 2, 0),
)
PASSES = (
    ((1, -1, 0), ((-2, 0), (0, -1), (0, 1))), ((1, 0, -1), ((1, 0), )), ((1, 0, 1), ()),
    ((0, 2, 0), ((0, 2), (1, 0), (0, -1), (0, 1))), ((0, 0, -1), ((1, 0), )), ((0, 0, 1), ((-1, 0), )),
    ((1, 1, 0), ((0, 1), )), ((0, -2, 0), ((-1, 0), (0, -1), (-2, 0), (0, 2))), ((0, 1, 0), ((0, 1), )),
    ((0, 0, 2), ()), ((1, 0, 2), ((2, 0), )), ((1, -2, 0), ((0, -1), )), ((1, 2, 0), ((1, 0), )),
    ((1, -1, -1), ((0, -1), )), ((1, -1, 1), ((-1, 0), )), ((1, 1, -1), ((1, 0), )),
    ((1, -3, 0), ((0, 1), (0, -1), (-1, 0))), ((0, 2, -1), ()), ((0, 2, 1), ()), ((0, 3, 0), ((0, 1), (0, -1))),
    ((0, -1, 1), ((0, 1), (-1, 0), (0, -1))), ((0, 2, 2), ((1, 0), (-1, 0))), ((0, 1, -1), ()),
    ((0, -3, 0), ((0, 1), )), ((0, -2, -1), ((-1, 0), (1, 0))), ((1, 1, 1), ((0, 1), (1, 0))),
    ((1, -2, -1), ((0, -1), )), ((0, 1, 1), ()), ((1, 2, 2), ((1, 0), )), ((0, 4, 0), ((0, 1), (0, -1))),
    ((0, -2, 2), ((-1, 0), )), ((1, 3, 0), ((0, 1), )), ((1, -2, 1), ()), ((1, -1, 2), ()),
    ((1, -3, 1), ((0, 1), (-1, 0))), ((1, 2, -1), ((1, 0), )), ((1, 4, 0), ((0, 2), )), ((1, -3, -1), ((-1, 0), )),
    ((0, 3, 1), ()), ((0, 3, 2), ((1, 0), )), ((0, -2, 1), ()), ((0, 3, -1), ()), ((0, -1, 2), ()),
    ((0, -1, -1), ()), ((0, 1, 2), ()), ((0, -1, 0), ()), ((0, -3, 1), ()), ((1, 2, 1), ()), ((0, -3, -1), ()),
    ((1, -2, 2), ()), ((1, 1, 2), ()), ((1, 3, 2), ()), ((0, -3, 2), ()), ((0, 4, -1), ()), ((0, 4, 1), ()),
    ((1, 4, 1), ()), ((1, 3, -1), ()), ((1, 3, 1), ()), ((1, 4, -1), ()), ((0, 4, 2), ()), ((1, 4, 2), ()),
    ((1, -3, 2), ()),
)


PEERS = sorted(
    [(z, x) for z in range(-3, 5) for x in range(-1, 3) if (z, x) != (0, 0)],
    key=lambda move: -abs(move[0]) - abs(move[1]),
)


def gather_kernel(
    hidden_hbm, gain_hbm, weight_hbm, conv_weight_hbm, conv_bias_hbm, proj_hbm, conv_state_hbm,
    act_out, mixed_out, step_out, bc_out,
    hidden, gain, conv_weight, conv_bias, proj, conv_state, raw, wide, ready, units, total, squares_x, squares_z, part, part_bc, got, got_bc,
    in_sem, weight_sem, recv_sem, send_sem, sq_sem, sum_sem, out_sem,
):
    req = lax.axis_index("req")
    me = lax.axis_index("chan")
    mz = me // XS
    mx = lax.rem(me, XS)

    def place(dz, dx):
        return lax.rem(mz + dz + ZS, ZS) * XS + lax.rem(mx + dx + XS, XS)

    small_copies = [
        pltpu.make_async_copy(source, target, in_sem.at[i])
        for i, (source, target) in enumerate(
            (
                (hidden_hbm, hidden),
                (gain_hbm, gain),
                (conv_weight_hbm, conv_weight),
                (conv_bias_hbm, conv_bias),
                (proj_hbm, proj),
                (conv_state_hbm, conv_state),
            )
        )
    ]
    small_copies[0].start()
    small_copies[1].start()
    weight_copies = [
        pltpu.make_async_copy(
            weight_hbm.at[pl.ds(i * 4096, 4096)], raw.at[pl.ds(i * 4096, 4096)], weight_sem.at[i]
        )
        for i in range(8)
    ]
    barrier = pltpu.get_barrier_semaphore()
    for hz, hx in GREETED:
        pl.semaphore_signal(barrier, inc=1, device_id=(req, place(-hz, -hx)), device_id_type=MESH)

    for copy in weight_copies:
        copy.start()
    for copy in small_copies[2:]:
        copy.start()
    small_copies[0].wait()
    small_copies[1].wait()
    widened = hidden[...].astype(F32)
    gain_rows = gain[...].astype(F32)
    for half in range(2):
        scaled = widened[:, half * 128 : half * 128 + 128] * gain_rows[half : half + 1]
        units[half, pl.ds(me, 1)] = scaled.astype(BF16)[None]
    square_row = lax.dot_general(
        jnp.ones((8, LOC), F32), widened * widened, (((1,), (1,)), ((), ())),
        precision=lax.Precision.HIGHEST, preferred_element_type=F32,
    )
    squares_x[pl.ds(mx, 1)] = square_row[None, :1]

    pl.semaphore_wait(barrier, len(GREETED))

    def push(half, z, x, hz, hx):
        owner = place(-z, -x)
        pltpu.make_async_remote_copy(
            units.at[half, owner], units.at[half, owner], send_sem.at[half],
            recv_sem.at[half, (z + hz) % ZS, (x + hx) % XS],
            device_id=(req, place(hz, hx)), device_id_type=MESH,
        ).start()

    def await_unit(half, z, x):
        owner = place(-z, -x)
        pltpu.make_async_copy(
            units.at[half, owner], units.at[half, owner], recv_sem.at[half, z % ZS, x % XS]
        ).wait()

    for half, hz, hx in OWN:
        push(half, 0, 0, hz, hx)
    for dx in (1, -1, 2):
        pltpu.make_async_remote_copy(
            squares_x.at[mx], squares_x.at[mx], sq_sem.at[0], sq_sem.at[1],
            device_id=(req, place(0, dx)), device_id_type=MESH,
        ).start()

    def convert(index, _):
        wide[...] = raw[pl.ds(pl.multiple_of(index * 1024, 1024), 1024), :].astype(F32)
        for side in range(2):
            for tile in range(2):
                column = side * 256 + tile * 128
                ready[pl.ds(pl.multiple_of(index * 256, 256), 256), column : column + 128] = wide[
                    pl.ds(2 * tile + side, 256, stride=4), :
                ].astype(BF16)
        return 0

    def multiply(z, x, first=False):
        owner = place(-z, -x)
        left = jnp.concatenate([units[0, owner], units[1, owner]], axis=1)
        product = jnp.dot(
            left, ready[pl.ds(pl.multiple_of(owner * 256, 256), 256), :], preferred_element_type=F32
        )
        total[...] = product if first else total[...] + product

    converted = 0

    def convert_to(count):
        nonlocal converted
        while converted < count:
            if converted % 4 == 0:
                weight_copies[converted // 4].wait()
            last = min(count, converted // 4 * 4 + 4)
            lax.fori_loop(converted, last, convert, 0)
            converted = last

    convert_to(8)
    arrived = {}
    pending = []
    started = False
    column = {0}
    for (half, z, x), moves in PASSES:
        await_unit(half, z, x)
        for hz, hx in moves:
            push(half, z, x, hz, hx)
        arrived[(z, x)] = arrived.get((z, x), 0) + 1
        if arrived[(z, x)] == 2:
            pending.append((z, x))
        if x == 0 and z not in column:
            column.add(z)
            if len(column) == ZS:
                pltpu.make_async_copy(
                    squares_x.at[pl.ds(0, 3)], squares_x.at[pl.ds(0, 3)], sq_sem.at[1]
                ).wait()
                squares_z[pl.ds(mz, 1)] = jnp.sum(squares_x[...], axis=0, keepdims=True)
                for hz in (1, -1, 2, -2, 3, -3, 4):
                    pltpu.make_async_remote_copy(
                        squares_z.at[mz], squares_z.at[mz], sq_sem.at[2], sq_sem.at[3],
                        device_id=(req, place(hz, 0)), device_id_type=MESH,
                    ).start()
        if converted < DEVS:
            convert_to(min(DEVS, converted + 2))
        elif pending:
            if not started:
                multiply(0, 0, True)
                started = True
            multiply(*pending.pop(0))
    while pending:
        multiply(*pending.pop(0))

    pltpu.make_async_copy(squares_z.at[pl.ds(0, 7)], squares_z.at[pl.ds(0, 7)], sq_sem.at[3]).wait()
    row = jnp.sum(squares_z[...], axis=0)
    inverse_row = lax.rsqrt(row / D + 1e-05)
    inverse = jnp.transpose(jnp.broadcast_to(inverse_row, (128, 128)))
    for copy in small_copies[2:]:
        copy.wait()
    mixed = [
        (total[:, i * 128 : i * 128 + 128] * inverse).astype(BF16) for i in range(4)
    ]
    new_inputs = jnp.concatenate(mixed[:2], axis=1)
    mixed_out[...] = jnp.concatenate(mixed, axis=1)
    window = conv_state[0].astype(F32) * conv_weight[0:1]
    window += conv_state[1].astype(F32) * conv_weight[1:2]
    window += conv_state[2].astype(F32) * conv_weight[2:3]
    window += new_inputs.astype(F32) * conv_weight[3:4]
    window += conv_bias[...]
    act = (window * jax.nn.sigmoid(window)).astype(BF16)
    act_out[...] = act
    projected = lax.dot_general(
        proj[...], act, (((1,), (1,)), ((), ())), preferred_element_type=F32
    )
    part[...] = projected[:DT_RANK].astype(BF16)
    for i in range(2 * N):
        part_bc[i] = projected[DT_RANK + i : DT_RANK + i + 1]

    def rows(index):
        return pl.ds(pl.multiple_of(index * 16, 16), 16)

    for hz, hx in PEERS:
        peer = place(hz, hx)
        pltpu.make_async_remote_copy(
            part.at[rows(peer)], got.at[rows(me)], sum_sem.at[0], sum_sem.at[1],
            device_id=(req, peer), device_id_type=MESH,
        ).start()
        pltpu.make_async_remote_copy(
            part_bc.at[peer], got_bc.at[me], sum_sem.at[2], sum_sem.at[3],
            device_id=(req, peer), device_id_type=MESH,
        ).start()
    got[rows(me), :] = part[rows(me), :]
    got_bc[pl.ds(me, 1)] = part_bc[pl.ds(me, 1)]

    some, some_bc = pl.ds(0, 31 * 16), pl.ds(0, 31)
    pltpu.make_async_copy(got.at[some], got.at[some], sum_sem.at[1]).wait()
    pltpu.make_async_copy(got_bc.at[some_bc], got_bc.at[some_bc], sum_sem.at[3]).wait()
    step = got[0:16].astype(F32)
    for i in range(1, DEVS):
        step += got[i * 16 : i * 16 + 16].astype(F32)
    step_out[rows(me), :] = step.astype(BF16)
    bc_out[pl.ds(me, 1)] = jnp.sum(got_bc[...], axis=0, keepdims=True)

    for hz, hx in PEERS:
        peer = place(hz, hx)
        pltpu.make_async_remote_copy(
            step_out.at[rows(me)], step_out.at[rows(me)], out_sem.at[0], out_sem.at[1],
            device_id=(req, peer), device_id_type=MESH,
        ).start()
        pltpu.make_async_remote_copy(
            bc_out.at[me], bc_out.at[me], out_sem.at[2], out_sem.at[3],
            device_id=(req, peer), device_id_type=MESH,
        ).start()
    for half in range(2):
        pltpu.make_async_copy(
            units.at[half, pl.ds(0, 31)], units.at[half, pl.ds(0, 31)], send_sem.at[half]
        ).wait()
    pltpu.make_async_copy(squares_x.at[pl.ds(0, 3)], squares_x.at[pl.ds(0, 3)], sq_sem.at[0]).wait()
    pltpu.make_async_copy(squares_z.at[pl.ds(0, 7)], squares_z.at[pl.ds(0, 7)], sq_sem.at[2]).wait()
    for i in (0, 2):
        pltpu.make_async_copy(
            (got if i == 0 else got_bc).at[some if i == 0 else some_bc],
            (got if i == 0 else got_bc).at[some if i == 0 else some_bc],
            sum_sem.at[i],
        ).wait()
    for i in range(4):
        ref, span = (step_out, some) if i < 2 else (bc_out, some_bc)
        pltpu.make_async_copy(ref.at[span], ref.at[span], out_sem.at[i]).wait()


def front(hidden, norm_gain, in_weight, conv_weight, conv_bias, x_proj_weight, conv_state):
    weight = in_weight.reshape(D, 2, 2, 128).transpose(0, 2, 1, 3).reshape(4 * D, 128)
    vmem = pl.BlockSpec(memory_space=pltpu.VMEM)
    return pl.pallas_call(
        gather_kernel,
        out_shape=(
            pltpu.VMEM((REQ, LOC), BF16),
            pltpu.VMEM((REQ, 2 * LOC), BF16),
            pltpu.VMEM((DT_RANK, REQ), BF16),
            pltpu.VMEM((2 * N, 1, REQ), F32),
        ),
        in_specs=[pl.BlockSpec(memory_space=pltpu.HBM)] * 7,
        out_specs=(vmem,) * 4,
        scratch_shapes=[
            pltpu.VMEM((REQ, LOC), BF16),
            pltpu.VMEM((2, 128), BF16),
            pltpu.VMEM((4, LOC), F32),
            pltpu.VMEM((1, LOC), F32),
            pltpu.VMEM((DT_RANK + 2 * N, LOC), BF16),
            pltpu.VMEM((3, REQ, LOC), BF16),
            pltpu.VMEM((4 * D, 128), BF16),
            pltpu.VMEM((1024, 128), F32),
            pltpu.VMEM((D, 2 * LOC), BF16),
            pltpu.VMEM((2, DEVS, REQ, 128), BF16),
            pltpu.VMEM((REQ, 2 * LOC), F32),
            pltpu.VMEM((XS, 1, REQ), F32),
            pltpu.VMEM((ZS, 1, REQ), F32),
            pltpu.VMEM((DT_RANK, REQ), BF16),
            pltpu.VMEM((2 * N, 1, REQ), F32),
            pltpu.VMEM((DT_RANK, REQ), BF16),
            pltpu.VMEM((DEVS, 1, REQ), F32),
            pltpu.SemaphoreType.DMA((6,)),
            pltpu.SemaphoreType.DMA((8,)),
            pltpu.SemaphoreType.DMA((2, ZS, XS)),
            pltpu.SemaphoreType.DMA((2,)),
            pltpu.SemaphoreType.DMA((4,)),
            pltpu.SemaphoreType.DMA((4,)),
            pltpu.SemaphoreType.DMA((4,)),
        ],
        compiler_params=pltpu.CompilerParams(
            collective_id=0, has_side_effects=True, vmem_limit_bytes=56 * 2**20
        ),
    )(
        hidden,
        norm_gain.reshape(2, 128),
        weight,
        conv_weight,
        conv_bias.reshape(1, LOC),
        x_proj_weight.T,
        conv_state.transpose(1, 0, 2),
    )


CHUNKS = 8
ROWS = REQ // CHUNKS


def state_kernel(
    act, mixed, step_raw, bc_raw, dt_gain, b_gain, c_gain, dt_weight, dt_bias, decay_log, skip_gain, conv_state, state,
    out_hbm, next_conv_hbm, next_state_hbm,
    step_size, drive, out, next_conv, next_state, sem,
):
    next_conv[0:2] = conv_state[1:3]
    next_conv[2] = mixed[:, :LOC]
    conv_copy = pltpu.make_async_copy(next_conv, next_conv_hbm, sem.at[CHUNKS])
    conv_copy.start()
    raw = step_raw[...].astype(F32)
    scale = lax.rsqrt(jnp.mean(raw * raw, axis=0, keepdims=True) + 1e-06)
    normed = (jnp.transpose(raw * scale) * dt_gain[...]).astype(BF16)
    before = jnp.dot(normed, dt_weight[...], preferred_element_type=F32) + dt_bias[...]
    size = jnp.maximum(before, 0.0) + jnp.log1p(jnp.exp(-jnp.abs(before)))
    step_size[...] = size
    drive[...] = size * act[...].astype(F32)
    square = (N, N)
    eye = lax.broadcasted_iota(jnp.int32, square, 0) == lax.broadcasted_iota(jnp.int32, square, 1)
    turned = []
    for part, gain_row in ((0, b_gain), (N, c_gain)):
        column = jnp.sum(
            jnp.where(eye, jnp.broadcast_to(gain_row[...], square), 0.0), axis=1, keepdims=True
        )
        values = bc_raw[part : part + N]
        scale = lax.rsqrt(jnp.mean(values * values, axis=0, keepdims=True) + 1e-06)
        turned.append(values * scale * column)
    b_turned, c_turned = turned
    rates = -jnp.exp(decay_log[...])
    copies = [conv_copy]
    for chunk in range(CHUNKS):
        rows = slice(chunk * ROWS, chunk * ROWS + ROWS)
        sums = []
        for r in range(chunk * ROWS, chunk * ROWS + ROWS):
            decay = jnp.exp(step_size[r : r + 1, :] * rates)
            new = decay * state[r].astype(F32) + drive[r : r + 1, :] * b_turned[:, r : r + 1]
            next_state[r] = new.astype(BF16)
            sums.append(jnp.sum(new * c_turned[:, r : r + 1], axis=0, keepdims=True))
        copies.append(
            pltpu.make_async_copy(next_state.at[rows], next_state_hbm.at[rows], sem.at[chunk])
        )
        copies[-1].start()
        summed = jnp.concatenate(sums, axis=0)
        act_wide = act[rows, :].astype(F32)
        gate = mixed[rows, LOC:].astype(F32)
        gated = (summed + skip_gain[...] * act_wide) * (gate * jax.nn.sigmoid(gate))
        out[rows, :] = gated.astype(BF16)
    copies.append(pltpu.make_async_copy(out, out_hbm, sem.at[CHUNKS + 1]))
    copies[-1].start()
    for copy in copies:
        copy.wait()


def local(
    hidden,
    norm_gain,
    in_weight,
    conv_weight,
    conv_bias,
    x_proj_weight,
    dt_norm_gain,
    b_norm_gain,
    c_norm_gain,
    dt_weight,
    dt_bias,
    decay_log,
    skip_gain,
    conv_state,
    ssm_state,
):
    act, mixed, step_raw, bc_raw = front(
        hidden, norm_gain, in_weight, conv_weight, conv_bias, x_proj_weight, conv_state
    )
    whole = pl.BlockSpec(memory_space=pltpu.VMEM)
    output, next_conv, next_state = pl.pallas_call(
        state_kernel,
        out_shape=(
            jax.ShapeDtypeStruct((REQ, LOC), BF16),
            jax.ShapeDtypeStruct((3, REQ, LOC), BF16),
            jax.ShapeDtypeStruct((REQ, N, LOC), BF16),
        ),
        in_specs=[whole] * 13,
        out_specs=(pl.BlockSpec(memory_space=pl.ANY),) * 3,
        scratch_shapes=[
            pltpu.VMEM((REQ, LOC), F32),
            pltpu.VMEM((REQ, LOC), F32),
            pltpu.VMEM((REQ, LOC), BF16),
            pltpu.VMEM((3, REQ, LOC), BF16),
            pltpu.VMEM((REQ, N, LOC), BF16),
            pltpu.SemaphoreType.DMA((CHUNKS + 2,)),
        ],
        compiler_params=pltpu.CompilerParams(vmem_limit_bytes=24 * 2**20),
    )(
        act,
        mixed,
        step_raw,
        bc_raw.reshape(2 * N, REQ),
        dt_norm_gain.reshape(1, DT_RANK),
        b_norm_gain.reshape(1, N),
        c_norm_gain.reshape(1, N),
        dt_weight,
        dt_bias.reshape(1, LOC),
        decay_log,
        skip_gain.reshape(1, LOC),
        conv_state.transpose(1, 0, 2),
        ssm_state,
    )
    return (output, next_conv.transpose(1, 0, 2), next_state)


def solution(mesh):
    return jax.shard_map(
        local,
        mesh=mesh,
        in_specs=(
            P("req", "chan"),
            P("chan"),
            P(None, None, "chan"),
            P(None, "chan"),
            P("chan"),
            P("chan", None),
            P(),
            P(),
            P(),
            P(None, "chan"),
            P("chan"),
            P(None, "chan"),
            P("chan"),
            P("req", None, "chan"),
            P("req", None, "chan"),
        ),
        out_specs=(P("req", "chan"), P("req", None, "chan"), P("req", None, "chan")),
        check_vma=False,
    )
```

```python
import jax
import jax.numpy as jnp
from jax import lax
from jax.experimental import pallas as pl
from jax.experimental.pallas import tpu as pltpu
from jax.sharding import PartitionSpec as P

D = 8192
N = 16
DT_RANK = 512
ZS = 8
XS = 4
DEVS = 32
REQ = 128
LOC = 256
MESH = pl.DeviceIdType.MESH
F32 = jnp.float32
BF16 = jnp.bfloat16

GREETED = ((-2, 0), (0, 2), (2, 0), (-1, 0), (0, -1), (0, 1), (1, 0))
OWN = (
    (1, -1, 0), (0, 2, 0), (1, 0, -1), (1, 0, 1), (0, 0, -1), (0, 0, 1), (0, -2, 0), (0, 0, 2), (1, -2, 0),
    (1, 0, 2), (1, 1, 0), (0, 1, 0), (1, 2, 0),
)
PASSES = (
    ((1, -1, 0), ((-2, 0), (0, -1), (0, 1))), ((1, 0, -1), ((1, 0), )), ((1, 0, 1), ()),
    ((0, 2, 0), ((0, 2), (1, 0), (0, -1), (0, 1))), ((0, 0, -1), ((1, 0), )), ((0, 0, 1), ((-1, 0), )),
    ((1, 1, 0), ((0, 1), )), ((0, -2, 0), ((-1, 0), (0, -1), (-2, 0), (0, 2))), ((0, 1, 0), ((0, 1), )),
    ((0, 0, 2), ()), ((1, 0, 2), ((2, 0), )), ((1, -2, 0), ((0, -1), )), ((1, 2, 0), ((1, 0), )),
    ((1, -1, -1), ((0, -1), )), ((1, -1, 1), ((-1, 0), )), ((1, 1, -1), ((1, 0), )),
    ((1, -3, 0), ((0, 1), (0, -1), (-1, 0))), ((0, 2, -1), ()), ((0, 2, 1), ()), ((0, 3, 0), ((0, 1), (0, -1))),
    ((0, -1, 1), ((0, 1), (-1, 0), (0, -1))), ((0, 2, 2), ((1, 0), (-1, 0))), ((0, 1, -1), ()),
    ((0, -3, 0), ((0, 1), )), ((0, -2, -1), ((-1, 0), (1, 0))), ((1, 1, 1), ((0, 1), (1, 0))),
    ((1, -2, -1), ((0, -1), )), ((0, 1, 1), ()), ((1, 2, 2), ((1, 0), )), ((0, 4, 0), ((0, 1), (0, -1))),
    ((0, -2, 2), ((-1, 0), )), ((1, 3, 0), ((0, 1), )), ((1, -2, 1), ()), ((1, -1, 2), ()),
    ((1, -3, 1), ((0, 1), (-1, 0))), ((1, 2, -1), ((1, 0), )), ((1, 4, 0), ((0, 2), )), ((1, -3, -1), ((-1, 0), )),
    ((0, 3, 1), ()), ((0, 3, 2), ((1, 0), )), ((0, -2, 1), ()), ((0, 3, -1), ()), ((0, -1, 2), ()),
    ((0, -1, -1), ()), ((0, 1, 2), ()), ((0, -1, 0), ()), ((0, -3, 1), ()), ((1, 2, 1), ()), ((0, -3, -1), ()),
    ((1, -2, 2), ()), ((1, 1, 2), ()), ((1, 3, 2), ()), ((0, -3, 2), ()), ((0, 4, -1), ()), ((0, 4, 1), ()),
    ((1, 4, 1), ()), ((1, 3, -1), ()), ((1, 3, 1), ()), ((1, 4, -1), ()), ((0, 4, 2), ()), ((1, 4, 2), ()),
    ((1, -3, 2), ()),
)


PEERS = sorted(
    [(z, x) for z in range(-3, 5) for x in range(-1, 3) if (z, x) != (0, 0)],
    key=lambda move: -abs(move[0]) - abs(move[1]),
)


def gather_kernel(
    hidden_hbm, gain_hbm, weight_hbm, conv_weight_hbm, conv_bias_hbm, proj_hbm, conv_state_hbm,
    act_out, mixed_out, step_out, bc_out,
    hidden, gain, conv_weight, conv_bias, proj, conv_state, raw, wide, ready, units, total, squares_x, squares_z, inverse, window, part, part_bc, got, got_bc,
    in_sem, weight_sem, recv_sem, send_sem, sq_sem, sum_sem, out_sem,
):
    req = lax.axis_index("req")
    me = lax.axis_index("chan")
    mz = me // XS
    mx = lax.rem(me, XS)

    def place(dz, dx):
        return lax.rem(mz + dz + ZS, ZS) * XS + lax.rem(mx + dx + XS, XS)

    small_copies = [
        pltpu.make_async_copy(source, target, in_sem.at[i])
        for i, (source, target) in enumerate(
            (
                (hidden_hbm, hidden),
                (gain_hbm, gain),
                (conv_weight_hbm, conv_weight),
                (conv_bias_hbm, conv_bias),
                (proj_hbm, proj),
                (conv_state_hbm, conv_state),
            )
        )
    ]
    small_copies[0].start()
    small_copies[1].start()
    weight_copies = [
        pltpu.make_async_copy(
            weight_hbm.at[pl.ds(i * 4096, 4096)], raw.at[pl.ds(i * 4096, 4096)], weight_sem.at[i]
        )
        for i in range(8)
    ]
    barrier = pltpu.get_barrier_semaphore()
    for hz, hx in GREETED:
        pl.semaphore_signal(barrier, inc=1, device_id=(req, place(-hz, -hx)), device_id_type=MESH)

    for copy in weight_copies:
        copy.start()
    for copy in small_copies[2:]:
        copy.start()
    small_copies[0].wait()
    small_copies[1].wait()
    widened = hidden[...].astype(F32)
    gain_rows = gain[...].astype(F32)
    for half in range(2):
        scaled = widened[:, half * 128 : half * 128 + 128] * gain_rows[half : half + 1]
        units[half, pl.ds(me, 1)] = scaled.astype(BF16)[None]
    square_row = lax.dot_general(
        jnp.ones((8, LOC), F32), widened * widened, (((1,), (1,)), ((), ())),
        precision=lax.Precision.HIGHEST, preferred_element_type=F32,
    )
    squares_x[pl.ds(mx, 1)] = square_row[None, :1]

    pl.semaphore_wait(barrier, len(GREETED))

    def push(half, z, x, hz, hx):
        owner = place(-z, -x)
        pltpu.make_async_remote_copy(
            units.at[half, owner], units.at[half, owner], send_sem.at[half],
            recv_sem.at[half, (z + hz) % ZS, (x + hx) % XS],
            device_id=(req, place(hz, hx)), device_id_type=MESH,
        ).start()

    def await_unit(half, z, x):
        owner = place(-z, -x)
        pltpu.make_async_copy(
            units.at[half, owner], units.at[half, owner], recv_sem.at[half, z % ZS, x % XS]
        ).wait()

    for half, hz, hx in OWN:
        push(half, 0, 0, hz, hx)
    for dx in (1, -1, 2):
        pltpu.make_async_remote_copy(
            squares_x.at[mx], squares_x.at[mx], sq_sem.at[0], sq_sem.at[1],
            device_id=(req, place(0, dx)), device_id_type=MESH,
        ).start()

    def convert(index, _):
        wide[...] = raw[pl.ds(pl.multiple_of(index * 1024, 1024), 1024), :].astype(F32)
        for side in range(2):
            for tile in range(2):
                column = side * 256 + tile * 128
                ready[pl.ds(pl.multiple_of(index * 256, 256), 256), column : column + 128] = wide[
                    pl.ds(2 * tile + side, 256, stride=4), :
                ].astype(BF16)
        return 0

    def multiply(z, x, first=False):
        owner = place(-z, -x)
        left = jnp.concatenate([units[0, owner], units[1, owner]], axis=1)
        product = jnp.dot(
            left, ready[pl.ds(pl.multiple_of(owner * 256, 256), 256), :], preferred_element_type=F32
        )
        total[...] = product if first else total[...] + product

    converted = 0

    def convert_to(count):
        nonlocal converted
        while converted < count:
            if converted % 4 == 0:
                weight_copies[converted // 4].wait()
            last = min(count, converted // 4 * 4 + 4)
            lax.fori_loop(converted, last, convert, 0)
            converted = last

    def settle():
        for copy in small_copies[2:]:
            copy.wait()
        pltpu.make_async_copy(
            squares_z.at[pl.ds(0, 7)], squares_z.at[pl.ds(0, 7)], sq_sem.at[3]
        ).wait()
        inverse_row = lax.rsqrt(jnp.sum(squares_z[...], axis=0) / D + 1e-05)
        inverse[...] = jnp.transpose(jnp.broadcast_to(inverse_row, (128, 128)))
        older = conv_state[0].astype(F32) * conv_weight[0:1]
        older += conv_state[1].astype(F32) * conv_weight[1:2]
        window[...] = older + conv_state[2].astype(F32) * conv_weight[2:3]

    convert_to(8)
    arrived = {}
    pending = []
    started = False
    column = {0}
    for step, ((half, z, x), moves) in enumerate(PASSES):
        await_unit(half, z, x)
        for hz, hx in moves:
            push(half, z, x, hz, hx)
        arrived[(z, x)] = arrived.get((z, x), 0) + 1
        if arrived[(z, x)] == 2:
            pending.append((z, x))
        if x == 0 and z not in column:
            column.add(z)
            if len(column) == ZS:
                pltpu.make_async_copy(
                    squares_x.at[pl.ds(0, 3)], squares_x.at[pl.ds(0, 3)], sq_sem.at[1]
                ).wait()
                squares_z[pl.ds(mz, 1)] = jnp.sum(squares_x[...], axis=0, keepdims=True)
                for hz in (1, -1, 2, -2, 3, -3, 4):
                    pltpu.make_async_remote_copy(
                        squares_z.at[mz], squares_z.at[mz], sq_sem.at[2], sq_sem.at[3],
                        device_id=(req, place(hz, 0)), device_id_type=MESH,
                    ).start()
        if converted < DEVS:
            convert_to(min(DEVS, converted + 2))
        elif pending:
            if not started:
                multiply(0, 0, True)
                started = True
            multiply(*pending.pop(0))
        if step == len(PASSES) - 5:
            settle()
    while pending:
        multiply(*pending.pop(0))

    mixed = [
        (total[:, i * 128 : i * 128 + 128] * inverse[...]).astype(BF16) for i in range(4)
    ]
    new_inputs = jnp.concatenate(mixed[:2], axis=1)
    mixed_out[...] = jnp.concatenate(mixed, axis=1)
    summed = window[...] + new_inputs.astype(F32) * conv_weight[3:4] + conv_bias[...]
    act = (summed * jax.nn.sigmoid(summed)).astype(BF16)
    act_out[...] = act
    projected = lax.dot_general(
        proj[...], act, (((1,), (1,)), ((), ())), preferred_element_type=F32
    )
    part[...] = projected[:DT_RANK].astype(BF16)
    for i in range(2 * N):
        part_bc[i] = projected[DT_RANK + i : DT_RANK + i + 1]

    def rows(index):
        return pl.ds(pl.multiple_of(index * 16, 16), 16)

    for hz, hx in PEERS:
        peer = place(hz, hx)
        pltpu.make_async_remote_copy(
            part.at[rows(peer)], got.at[rows(me)], sum_sem.at[0], sum_sem.at[1],
            device_id=(req, peer), device_id_type=MESH,
        ).start()
        pltpu.make_async_remote_copy(
            part_bc.at[peer], got_bc.at[me], sum_sem.at[2], sum_sem.at[3],
            device_id=(req, peer), device_id_type=MESH,
        ).start()
    got[rows(me), :] = part[rows(me), :]
    got_bc[pl.ds(me, 1)] = part_bc[pl.ds(me, 1)]

    some, some_bc = pl.ds(0, 31 * 16), pl.ds(0, 31)
    pltpu.make_async_copy(got.at[some], got.at[some], sum_sem.at[1]).wait()
    pltpu.make_async_copy(got_bc.at[some_bc], got_bc.at[some_bc], sum_sem.at[3]).wait()
    reduced = got[0:16].astype(F32)
    for i in range(1, DEVS):
        reduced += got[i * 16 : i * 16 + 16].astype(F32)
    step_out[rows(me), :] = reduced.astype(BF16)
    bc_out[pl.ds(me, 1)] = jnp.sum(got_bc[...], axis=0, keepdims=True)

    for hz, hx in PEERS:
        peer = place(hz, hx)
        pltpu.make_async_remote_copy(
            step_out.at[rows(me)], step_out.at[rows(me)], out_sem.at[0], out_sem.at[1],
            device_id=(req, peer), device_id_type=MESH,
        ).start()
        pltpu.make_async_remote_copy(
            bc_out.at[me], bc_out.at[me], out_sem.at[2], out_sem.at[3],
            device_id=(req, peer), device_id_type=MESH,
        ).start()
    for half in range(2):
        pltpu.make_async_copy(
            units.at[half, pl.ds(0, 31)], units.at[half, pl.ds(0, 31)], send_sem.at[half]
        ).wait()
    pltpu.make_async_copy(squares_x.at[pl.ds(0, 3)], squares_x.at[pl.ds(0, 3)], sq_sem.at[0]).wait()
    pltpu.make_async_copy(squares_z.at[pl.ds(0, 7)], squares_z.at[pl.ds(0, 7)], sq_sem.at[2]).wait()
    for i in (0, 2):
        pltpu.make_async_copy(
            (got if i == 0 else got_bc).at[some if i == 0 else some_bc],
            (got if i == 0 else got_bc).at[some if i == 0 else some_bc],
            sum_sem.at[i],
        ).wait()
    for i in range(4):
        ref, span = (step_out, some) if i < 2 else (bc_out, some_bc)
        pltpu.make_async_copy(ref.at[span], ref.at[span], out_sem.at[i]).wait()


def front(hidden, norm_gain, in_weight, conv_weight, conv_bias, x_proj_weight, conv_state):
    weight = in_weight.reshape(D, 2, 2, 128).transpose(0, 2, 1, 3).reshape(4 * D, 128)
    vmem = pl.BlockSpec(memory_space=pltpu.VMEM)
    return pl.pallas_call(
        gather_kernel,
        out_shape=(
            pltpu.VMEM((REQ, LOC), BF16),
            pltpu.VMEM((REQ, 2 * LOC), BF16),
            pltpu.VMEM((DT_RANK, REQ), BF16),
            pltpu.VMEM((2 * N, 1, REQ), F32),
        ),
        in_specs=[pl.BlockSpec(memory_space=pltpu.HBM)] * 7,
        out_specs=(vmem,) * 4,
        scratch_shapes=[
            pltpu.VMEM((REQ, LOC), BF16),
            pltpu.VMEM((2, 128), BF16),
            pltpu.VMEM((4, LOC), F32),
            pltpu.VMEM((1, LOC), F32),
            pltpu.VMEM((DT_RANK + 2 * N, LOC), BF16),
            pltpu.VMEM((3, REQ, LOC), BF16),
            pltpu.VMEM((4 * D, 128), BF16),
            pltpu.VMEM((1024, 128), F32),
            pltpu.VMEM((D, 2 * LOC), BF16),
            pltpu.VMEM((2, DEVS, REQ, 128), BF16),
            pltpu.VMEM((REQ, 2 * LOC), F32),
            pltpu.VMEM((XS, 1, REQ), F32),
            pltpu.VMEM((ZS, 1, REQ), F32),
            pltpu.VMEM((128, 128), F32),
            pltpu.VMEM((REQ, LOC), F32),
            pltpu.VMEM((DT_RANK, REQ), BF16),
            pltpu.VMEM((2 * N, 1, REQ), F32),
            pltpu.VMEM((DT_RANK, REQ), BF16),
            pltpu.VMEM((DEVS, 1, REQ), F32),
            pltpu.SemaphoreType.DMA((6,)),
            pltpu.SemaphoreType.DMA((8,)),
            pltpu.SemaphoreType.DMA((2, ZS, XS)),
            pltpu.SemaphoreType.DMA((2,)),
            pltpu.SemaphoreType.DMA((4,)),
            pltpu.SemaphoreType.DMA((4,)),
            pltpu.SemaphoreType.DMA((4,)),
        ],
        compiler_params=pltpu.CompilerParams(
            collective_id=0, has_side_effects=True, vmem_limit_bytes=56 * 2**20
        ),
    )(
        hidden,
        norm_gain.reshape(2, 128),
        weight,
        conv_weight,
        conv_bias.reshape(1, LOC),
        x_proj_weight.T,
        conv_state.transpose(1, 0, 2),
    )


CHUNKS = 8
ROWS = REQ // CHUNKS


def state_kernel(
    act, mixed, step_raw, bc_raw, dt_gain, b_gain, c_gain, dt_weight, dt_bias, decay_log, skip_gain, conv_state, state,
    out_hbm, next_conv_hbm, next_state_hbm,
    step_size, drive, out, next_conv, next_state, sem,
):
    next_conv[0:2] = conv_state[1:3]
    next_conv[2] = mixed[:, :LOC]
    conv_copy = pltpu.make_async_copy(next_conv, next_conv_hbm, sem.at[CHUNKS])
    conv_copy.start()
    raw = step_raw[...].astype(F32)
    scale = lax.rsqrt(jnp.mean(raw * raw, axis=0, keepdims=True) + 1e-06)
    normed = (jnp.transpose(raw * scale) * dt_gain[...]).astype(BF16)
    before = jnp.dot(normed, dt_weight[...], preferred_element_type=F32) + dt_bias[...]
    size = jnp.maximum(before, 0.0) + jnp.log1p(jnp.exp(-jnp.abs(before)))
    step_size[...] = size
    drive[...] = size * act[...].astype(F32)
    square = (N, N)
    eye = lax.broadcasted_iota(jnp.int32, square, 0) == lax.broadcasted_iota(jnp.int32, square, 1)
    turned = []
    for part, gain_row in ((0, b_gain), (N, c_gain)):
        column = jnp.sum(
            jnp.where(eye, jnp.broadcast_to(gain_row[...], square), 0.0), axis=1, keepdims=True
        )
        values = bc_raw[part : part + N]
        scale = lax.rsqrt(jnp.mean(values * values, axis=0, keepdims=True) + 1e-06)
        turned.append(values * scale * column)
    b_turned, c_turned = turned
    rates = -jnp.exp(decay_log[...])
    copies = [conv_copy]
    for chunk in range(CHUNKS):
        rows = slice(chunk * ROWS, chunk * ROWS + ROWS)
        sums = []
        for r in range(chunk * ROWS, chunk * ROWS + ROWS):
            decay = jnp.exp(step_size[r : r + 1, :] * rates)
            new = decay * state[r].astype(F32) + drive[r : r + 1, :] * b_turned[:, r : r + 1]
            next_state[r] = new.astype(BF16)
            sums.append(jnp.sum(new * c_turned[:, r : r + 1], axis=0, keepdims=True))
        copies.append(
            pltpu.make_async_copy(next_state.at[rows], next_state_hbm.at[rows], sem.at[chunk])
        )
        copies[-1].start()
        summed = jnp.concatenate(sums, axis=0)
        act_wide = act[rows, :].astype(F32)
        gate = mixed[rows, LOC:].astype(F32)
        gated = (summed + skip_gain[...] * act_wide) * (gate * jax.nn.sigmoid(gate))
        out[rows, :] = gated.astype(BF16)
    copies.append(pltpu.make_async_copy(out, out_hbm, sem.at[CHUNKS + 1]))
    copies[-1].start()
    for copy in copies:
        copy.wait()


def local(
    hidden,
    norm_gain,
    in_weight,
    conv_weight,
    conv_bias,
    x_proj_weight,
    dt_norm_gain,
    b_norm_gain,
    c_norm_gain,
    dt_weight,
    dt_bias,
    decay_log,
    skip_gain,
    conv_state,
    ssm_state,
):
    act, mixed, step_raw, bc_raw = front(
        hidden, norm_gain, in_weight, conv_weight, conv_bias, x_proj_weight, conv_state
    )
    whole = pl.BlockSpec(memory_space=pltpu.VMEM)
    output, next_conv, next_state = pl.pallas_call(
        state_kernel,
        out_shape=(
            jax.ShapeDtypeStruct((REQ, LOC), BF16),
            jax.ShapeDtypeStruct((3, REQ, LOC), BF16),
            jax.ShapeDtypeStruct((REQ, N, LOC), BF16),
        ),
        in_specs=[whole] * 13,
        out_specs=(pl.BlockSpec(memory_space=pl.ANY),) * 3,
        scratch_shapes=[
            pltpu.VMEM((REQ, LOC), F32),
            pltpu.VMEM((REQ, LOC), F32),
            pltpu.VMEM((REQ, LOC), BF16),
            pltpu.VMEM((3, REQ, LOC), BF16),
            pltpu.VMEM((REQ, N, LOC), BF16),
            pltpu.SemaphoreType.DMA((CHUNKS + 2,)),
        ],
        compiler_params=pltpu.CompilerParams(vmem_limit_bytes=24 * 2**20),
    )(
        act,
        mixed,
        step_raw,
        bc_raw.reshape(2 * N, REQ),
        dt_norm_gain.reshape(1, DT_RANK),
        b_norm_gain.reshape(1, N),
        c_norm_gain.reshape(1, N),
        dt_weight,
        dt_bias.reshape(1, LOC),
        decay_log,
        skip_gain.reshape(1, LOC),
        conv_state.transpose(1, 0, 2),
        ssm_state,
    )
    return (output, next_conv.transpose(1, 0, 2), next_state)


def solution(mesh):
    return jax.shard_map(
        local,
        mesh=mesh,
        in_specs=(
            P("req", "chan"),
            P("chan"),
            P(None, None, "chan"),
            P(None, "chan"),
            P("chan"),
            P("chan", None),
            P(),
            P(),
            P(),
            P(None, "chan"),
            P("chan"),
            P(None, "chan"),
            P("chan"),
            P("req", None, "chan"),
            P("req", None, "chan"),
        ),
        out_specs=(P("req", "chan"), P("req", None, "chan"), P("req", None, "chan")),
        check_vma=False,
    )
```

```python
import jax
import jax.numpy as jnp
from jax import lax
from jax.experimental import pallas as pl
from jax.experimental.pallas import tpu as pltpu
from jax.sharding import PartitionSpec as P

D = 8192
N = 16
DT_RANK = 512
ZS = 8
XS = 4
DEVS = 32
REQ = 128
LOC = 256
MESH = pl.DeviceIdType.MESH
F32 = jnp.float32
BF16 = jnp.bfloat16

GREETED = ((-2, 0), (0, 2), (2, 0), (-1, 0), (0, -1), (0, 1), (1, 0))
OWN = (
    (1, -1, 0), (0, 2, 0), (1, 0, -1), (1, 0, 1), (0, 0, -1), (0, 0, 1), (0, -2, 0), (0, 0, 2), (1, -2, 0),
    (1, 0, 2), (1, 1, 0), (0, 1, 0), (1, 2, 0),
)
PASSES = (
    ((1, -1, 0), ((-2, 0), (0, -1), (0, 1))), ((1, 0, -1), ((1, 0), )), ((1, 0, 1), ()),
    ((0, 2, 0), ((0, 2), (1, 0), (0, -1), (0, 1))), ((0, 0, -1), ((1, 0), )), ((0, 0, 1), ((-1, 0), )),
    ((1, 1, 0), ((0, 1), )), ((0, -2, 0), ((-1, 0), (0, -1), (-2, 0), (0, 2))), ((0, 1, 0), ((0, 1), )),
    ((0, 0, 2), ()), ((1, 0, 2), ((2, 0), )), ((1, -2, 0), ((0, -1), )), ((1, 2, 0), ((1, 0), )),
    ((1, -1, -1), ((0, -1), )), ((1, -1, 1), ((-1, 0), )), ((1, 1, -1), ((1, 0), )),
    ((1, -3, 0), ((0, 1), (0, -1), (-1, 0))), ((0, 2, -1), ()), ((0, 2, 1), ()), ((0, 3, 0), ((0, 1), (0, -1))),
    ((0, -1, 1), ((0, 1), (-1, 0), (0, -1))), ((0, 2, 2), ((1, 0), (-1, 0))), ((0, 1, -1), ()),
    ((0, -3, 0), ((0, 1), )), ((0, -2, -1), ((-1, 0), (1, 0))), ((1, 1, 1), ((0, 1), (1, 0))),
    ((1, -2, -1), ((0, -1), )), ((0, 1, 1), ()), ((1, 2, 2), ((1, 0), )), ((0, 4, 0), ((0, 1), (0, -1))),
    ((0, -2, 2), ((-1, 0), )), ((1, 3, 0), ((0, 1), )), ((1, -2, 1), ()), ((1, -1, 2), ()),
    ((1, -3, 1), ((0, 1), (-1, 0))), ((1, 2, -1), ((1, 0), )), ((1, 4, 0), ((0, 2), )), ((1, -3, -1), ((-1, 0), )),
    ((0, 3, 1), ()), ((0, 3, 2), ((1, 0), )), ((0, -2, 1), ()), ((0, 3, -1), ()), ((0, -1, 2), ()),
    ((0, -1, -1), ()), ((0, 1, 2), ()), ((0, -1, 0), ()), ((0, -3, 1), ()), ((1, 2, 1), ()), ((0, -3, -1), ()),
    ((1, -2, 2), ()), ((1, 1, 2), ()), ((1, 3, 2), ()), ((0, -3, 2), ()), ((0, 4, -1), ()), ((0, 4, 1), ()),
    ((1, 4, 1), ()), ((1, 3, -1), ()), ((1, 3, 1), ()), ((1, 4, -1), ()), ((0, 4, 2), ()), ((1, 4, 2), ()),
    ((1, -3, 2), ()),
)


PEERS = sorted(
    [(z, x) for z in range(-3, 5) for x in range(-1, 3) if (z, x) != (0, 0)],
    key=lambda move: -abs(move[0]) - abs(move[1]),
)


def gather_kernel(
    hidden_hbm, gain_hbm, weight_hbm, conv_weight_hbm, conv_bias_hbm, proj_hbm, conv_state_hbm,
    act_out, mixed_out, step_out, bc_out,
    hidden, gain, conv_weight, conv_bias, proj, conv_state, raw, wide, ready, units, total, squares_x, squares_z, inverse, window, part, part_bc, got, got_bc,
    in_sem, weight_sem, recv_sem, send_sem, sq_sem, sum_sem, out_sem,
):
    req = lax.axis_index("req")
    me = lax.axis_index("chan")
    mz = me // XS
    mx = lax.rem(me, XS)

    def place(dz, dx):
        return lax.rem(mz + dz + ZS, ZS) * XS + lax.rem(mx + dx + XS, XS)

    small_copies = [
        pltpu.make_async_copy(source, target, in_sem.at[i])
        for i, (source, target) in enumerate(
            (
                (hidden_hbm, hidden),
                (gain_hbm, gain),
                (conv_weight_hbm, conv_weight),
                (conv_bias_hbm, conv_bias),
                (proj_hbm, proj),
                (conv_state_hbm, conv_state),
            )
        )
    ]
    small_copies[0].start()
    small_copies[1].start()
    weight_copies = [
        pltpu.make_async_copy(
            weight_hbm.at[pl.ds(i * 4096, 4096)], raw.at[pl.ds(i * 4096, 4096)], weight_sem.at[i]
        )
        for i in range(8)
    ]
    barrier = pltpu.get_barrier_semaphore()
    for hz, hx in GREETED:
        pl.semaphore_signal(barrier, inc=1, device_id=(req, place(-hz, -hx)), device_id_type=MESH)

    for copy in weight_copies:
        copy.start()
    for copy in small_copies[2:]:
        copy.start()
    small_copies[0].wait()
    small_copies[1].wait()
    widened = hidden[...].astype(F32)
    gain_rows = gain[...].astype(F32)
    for half in range(2):
        scaled = widened[:, half * 128 : half * 128 + 128] * gain_rows[half : half + 1]
        units[half, pl.ds(me, 1)] = scaled.astype(BF16)[None]
    square_row = lax.dot_general(
        jnp.ones((8, LOC), F32), widened * widened, (((1,), (1,)), ((), ())),
        precision=lax.Precision.HIGHEST, preferred_element_type=F32,
    )
    squares_x[pl.ds(mx, 1)] = square_row[None, :1]

    pl.semaphore_wait(barrier, len(GREETED))

    def push(half, z, x, hz, hx):
        owner = place(-z, -x)
        pltpu.make_async_remote_copy(
            units.at[half, owner], units.at[half, owner], send_sem.at[half],
            recv_sem.at[half, (z + hz) % ZS, (x + hx) % XS],
            device_id=(req, place(hz, hx)), device_id_type=MESH,
        ).start()

    def await_unit(half, z, x):
        owner = place(-z, -x)
        pltpu.make_async_copy(
            units.at[half, owner], units.at[half, owner], recv_sem.at[half, z % ZS, x % XS]
        ).wait()

    for half, hz, hx in OWN:
        push(half, 0, 0, hz, hx)
    for dx in (1, -1, 2):
        pltpu.make_async_remote_copy(
            squares_x.at[mx], squares_x.at[mx], sq_sem.at[0], sq_sem.at[1],
            device_id=(req, place(0, dx)), device_id_type=MESH,
        ).start()

    def convert(index, _):
        wide[...] = raw[pl.ds(pl.multiple_of(index * 1024, 1024), 1024), :].astype(F32)
        for side in range(2):
            for tile in range(2):
                column = side * 256 + tile * 128
                ready[pl.ds(pl.multiple_of(index * 256, 256), 256), column : column + 128] = wide[
                    pl.ds(2 * tile + side, 256, stride=4), :
                ].astype(BF16)
        return 0

    def multiply(z, x, first=False):
        owner = place(-z, -x)
        left = jnp.concatenate([units[0, owner], units[1, owner]], axis=1)
        product = jnp.dot(
            left, ready[pl.ds(pl.multiple_of(owner * 256, 256), 256), :], preferred_element_type=F32
        )
        total[...] = product if first else total[...] + product

    converted = 0

    def convert_to(count):
        nonlocal converted
        while converted < count:
            if converted % 4 == 0:
                weight_copies[converted // 4].wait()
            last = min(count, converted // 4 * 4 + 4)
            lax.fori_loop(converted, last, convert, 0)
            converted = last

    def settle():
        for copy in small_copies[2:]:
            copy.wait()
        pltpu.make_async_copy(
            squares_z.at[pl.ds(0, 7)], squares_z.at[pl.ds(0, 7)], sq_sem.at[3]
        ).wait()
        inverse_row = lax.rsqrt(jnp.sum(squares_z[...], axis=0) / D + 1e-05)
        inverse[...] = jnp.transpose(jnp.broadcast_to(inverse_row, (128, 128)))
        older = conv_state[0].astype(F32) * conv_weight[0:1]
        older += conv_state[1].astype(F32) * conv_weight[1:2]
        window[...] = older + conv_state[2].astype(F32) * conv_weight[2:3]

    convert_to(8)
    arrived = {}
    pending = []
    started = False
    column = {0}
    for step, ((half, z, x), moves) in enumerate(PASSES):
        await_unit(half, z, x)
        for hz, hx in moves:
            push(half, z, x, hz, hx)
        arrived[(z, x)] = arrived.get((z, x), 0) + 1
        if arrived[(z, x)] == 2:
            pending.append((z, x))
        if x == 0 and z not in column:
            column.add(z)
            if len(column) == ZS:
                pltpu.make_async_copy(
                    squares_x.at[pl.ds(0, 3)], squares_x.at[pl.ds(0, 3)], sq_sem.at[1]
                ).wait()
                squares_z[pl.ds(mz, 1)] = jnp.sum(squares_x[...], axis=0, keepdims=True)
                for hz in (1, -1, 2, -2, 3, -3, 4):
                    pltpu.make_async_remote_copy(
                        squares_z.at[mz], squares_z.at[mz], sq_sem.at[2], sq_sem.at[3],
                        device_id=(req, place(hz, 0)), device_id_type=MESH,
                    ).start()
        if converted < DEVS:
            convert_to(min(DEVS, converted + 2))
        elif pending:
            if not started:
                multiply(0, 0, True)
                started = True
            multiply(*pending.pop(0))
        if step == len(PASSES) - 5:
            settle()
    while pending:
        multiply(*pending.pop(0))

    mixed = [
        (total[:, i * 128 : i * 128 + 128] * inverse[...]).astype(BF16) for i in range(4)
    ]
    new_inputs = jnp.concatenate(mixed[:2], axis=1)
    mixed_out[...] = jnp.concatenate(mixed, axis=1)
    summed = window[...] + new_inputs.astype(F32) * conv_weight[3:4] + conv_bias[...]
    act = (summed * jax.nn.sigmoid(summed)).astype(BF16)
    act_out[...] = act
    projected = lax.dot_general(
        proj[...], act, (((1,), (1,)), ((), ())), preferred_element_type=F32
    )
    part[...] = projected[:DT_RANK].astype(BF16)
    for i in range(2 * N):
        part_bc[i] = projected[DT_RANK + i : DT_RANK + i + 1]

    def rows(index):
        return pl.ds(pl.multiple_of(index * 16, 16), 16)

    for hz, hx in PEERS:
        peer = place(hz, hx)
        pltpu.make_async_remote_copy(
            part.at[rows(peer)], got.at[rows(me)], sum_sem.at[0], sum_sem.at[1],
            device_id=(req, peer), device_id_type=MESH,
        ).start()
        pltpu.make_async_remote_copy(
            part_bc.at[peer], got_bc.at[me], sum_sem.at[2], sum_sem.at[3],
            device_id=(req, peer), device_id_type=MESH,
        ).start()
    got[rows(me), :] = part[rows(me), :]
    got_bc[pl.ds(me, 1)] = part_bc[pl.ds(me, 1)]

    some, some_bc = pl.ds(0, 31 * 16), pl.ds(0, 31)
    pltpu.make_async_copy(got.at[some], got.at[some], sum_sem.at[1]).wait()
    pltpu.make_async_copy(got_bc.at[some_bc], got_bc.at[some_bc], sum_sem.at[3]).wait()
    reduced = got[0:16].astype(F32)
    for i in range(1, DEVS):
        reduced += got[i * 16 : i * 16 + 16].astype(F32)
    step_out[rows(me), :] = reduced.astype(BF16)
    bc_out[pl.ds(me, 1)] = jnp.sum(got_bc[...], axis=0, keepdims=True)

    for hz, hx in PEERS:
        peer = place(hz, hx)
        pltpu.make_async_remote_copy(
            step_out.at[rows(me)], step_out.at[rows(me)], out_sem.at[0], out_sem.at[1],
            device_id=(req, peer), device_id_type=MESH,
        ).start()
        pltpu.make_async_remote_copy(
            bc_out.at[me], bc_out.at[me], out_sem.at[2], out_sem.at[3],
            device_id=(req, peer), device_id_type=MESH,
        ).start()
    for half in range(2):
        pltpu.make_async_copy(
            units.at[half, pl.ds(0, 31)], units.at[half, pl.ds(0, 31)], send_sem.at[half]
        ).wait()
    pltpu.make_async_copy(squares_x.at[pl.ds(0, 3)], squares_x.at[pl.ds(0, 3)], sq_sem.at[0]).wait()
    pltpu.make_async_copy(squares_z.at[pl.ds(0, 7)], squares_z.at[pl.ds(0, 7)], sq_sem.at[2]).wait()
    for i in (0, 2):
        pltpu.make_async_copy(
            (got if i == 0 else got_bc).at[some if i == 0 else some_bc],
            (got if i == 0 else got_bc).at[some if i == 0 else some_bc],
            sum_sem.at[i],
        ).wait()
    for i in range(4):
        ref, span = (step_out, some) if i < 2 else (bc_out, some_bc)
        pltpu.make_async_copy(ref.at[span], ref.at[span], out_sem.at[i]).wait()


def front(hidden, norm_gain, in_weight, conv_weight, conv_bias, x_proj_weight, conv_state):
    weight = in_weight.reshape(D, 2, 2, 128).transpose(0, 2, 1, 3).reshape(4 * D, 128)
    vmem = pl.BlockSpec(memory_space=pltpu.VMEM)
    return pl.pallas_call(
        gather_kernel,
        out_shape=(
            pltpu.VMEM((REQ, LOC), BF16),
            pltpu.VMEM((REQ, 2 * LOC), BF16),
            pltpu.VMEM((DT_RANK, REQ), BF16),
            pltpu.VMEM((2 * N, 1, REQ), F32),
        ),
        in_specs=[pl.BlockSpec(memory_space=pltpu.HBM)] * 7,
        out_specs=(vmem,) * 4,
        scratch_shapes=[
            pltpu.VMEM((REQ, LOC), BF16),
            pltpu.VMEM((2, 128), BF16),
            pltpu.VMEM((4, LOC), F32),
            pltpu.VMEM((1, LOC), F32),
            pltpu.VMEM((DT_RANK + 2 * N, LOC), BF16),
            pltpu.VMEM((3, REQ, LOC), BF16),
            pltpu.VMEM((4 * D, 128), BF16),
            pltpu.VMEM((1024, 128), F32),
            pltpu.VMEM((D, 2 * LOC), BF16),
            pltpu.VMEM((2, DEVS, REQ, 128), BF16),
            pltpu.VMEM((REQ, 2 * LOC), F32),
            pltpu.VMEM((XS, 1, REQ), F32),
            pltpu.VMEM((ZS, 1, REQ), F32),
            pltpu.VMEM((128, 128), F32),
            pltpu.VMEM((REQ, LOC), F32),
            pltpu.VMEM((DT_RANK, REQ), BF16),
            pltpu.VMEM((2 * N, 1, REQ), F32),
            pltpu.VMEM((DT_RANK, REQ), BF16),
            pltpu.VMEM((DEVS, 1, REQ), F32),
            pltpu.SemaphoreType.DMA((6,)),
            pltpu.SemaphoreType.DMA((8,)),
            pltpu.SemaphoreType.DMA((2, ZS, XS)),
            pltpu.SemaphoreType.DMA((2,)),
            pltpu.SemaphoreType.DMA((4,)),
            pltpu.SemaphoreType.DMA((4,)),
            pltpu.SemaphoreType.DMA((4,)),
        ],
        compiler_params=pltpu.CompilerParams(
            collective_id=0, has_side_effects=True, vmem_limit_bytes=56 * 2**20
        ),
    )(
        hidden,
        norm_gain.reshape(2, 128),
        weight,
        conv_weight,
        conv_bias.reshape(1, LOC),
        x_proj_weight.T,
        conv_state.transpose(1, 0, 2),
    )


CHUNKS = 8
ROWS = REQ // CHUNKS


def state_kernel(
    act, mixed, step_raw, bc_raw, dt_gain, b_gain, c_gain, dt_weight, dt_bias, decay_log, skip_gain, conv_state, state,
    out_hbm, next_conv_hbm, next_state_hbm,
    step_size, drive, folded, out, next_conv, next_state, sem,
):
    next_conv[0:2] = conv_state[1:3]
    next_conv[2] = mixed[:, :LOC]
    conv_copy = pltpu.make_async_copy(next_conv, next_conv_hbm, sem.at[CHUNKS])
    conv_copy.start()
    raw = step_raw[...].astype(F32)
    scale = lax.rsqrt(jnp.mean(raw * raw, axis=0, keepdims=True) + 1e-06)
    normed = (jnp.transpose(raw * scale) * dt_gain[...]).astype(BF16)
    before = jnp.dot(normed, dt_weight[...], preferred_element_type=F32) + dt_bias[...]
    size = jnp.maximum(before, 0.0) + jnp.log1p(jnp.exp(-jnp.abs(before)))
    step_size[...] = size
    drive[...] = size * act[...].astype(F32)
    square = (N, N)
    eye = lax.broadcasted_iota(jnp.int32, square, 0) == lax.broadcasted_iota(jnp.int32, square, 1)
    turned = []
    for part, gain_row in ((0, b_gain), (N, c_gain)):
        column = jnp.sum(
            jnp.where(eye, jnp.broadcast_to(gain_row[...], square), 0.0), axis=1, keepdims=True
        )
        values = bc_raw[part : part + N]
        scale = lax.rsqrt(jnp.mean(values * values, axis=0, keepdims=True) + 1e-06)
        turned.append(values * scale * column)
    b_turned, c_turned = turned
    rates = -jnp.exp(decay_log[...])
    copies = [conv_copy]
    for chunk in range(CHUNKS):
        rows = slice(chunk * ROWS, chunk * ROWS + ROWS)
        for r in range(chunk * ROWS, chunk * ROWS + ROWS):
            decay = jnp.exp(step_size[r : r + 1, :] * rates)
            new = decay * state[r].astype(F32) + drive[r : r + 1, :] * b_turned[:, r : r + 1]
            next_state[r] = new.astype(BF16)
            weighted = new * c_turned[:, r : r + 1]
            for tile in range(2):
                lanes = slice(tile * 128, tile * 128 + 128)
                folded[tile, r * 8 : r * 8 + 8] = weighted[:8, lanes] + weighted[8:, lanes]
        copies.append(
            pltpu.make_async_copy(next_state.at[rows], next_state_hbm.at[rows], sem.at[chunk])
        )
        copies[-1].start()
        first = chunk * ROWS * 8
        halves = []
        for tile in range(2):
            half = folded[tile, pl.ds(first, ROWS, stride=8), :]
            for i in range(1, 8):
                half += folded[tile, pl.ds(first + i, ROWS, stride=8), :]
            halves.append(half)
        summed = jnp.concatenate(halves, axis=1)
        act_wide = act[rows, :].astype(F32)
        gate = mixed[rows, LOC:].astype(F32)
        gated = (summed + skip_gain[...] * act_wide) * (gate * jax.nn.sigmoid(gate))
        out[rows, :] = gated.astype(BF16)
    copies.append(pltpu.make_async_copy(out, out_hbm, sem.at[CHUNKS + 1]))
    copies[-1].start()
    for copy in copies:
        copy.wait()


def local(
    hidden,
    norm_gain,
    in_weight,
    conv_weight,
    conv_bias,
    x_proj_weight,
    dt_norm_gain,
    b_norm_gain,
    c_norm_gain,
    dt_weight,
    dt_bias,
    decay_log,
    skip_gain,
    conv_state,
    ssm_state,
):
    act, mixed, step_raw, bc_raw = front(
        hidden, norm_gain, in_weight, conv_weight, conv_bias, x_proj_weight, conv_state
    )
    whole = pl.BlockSpec(memory_space=pltpu.VMEM)
    output, next_conv, next_state = pl.pallas_call(
        state_kernel,
        out_shape=(
            jax.ShapeDtypeStruct((REQ, LOC), BF16),
            jax.ShapeDtypeStruct((3, REQ, LOC), BF16),
            jax.ShapeDtypeStruct((REQ, N, LOC), BF16),
        ),
        in_specs=[whole] * 13,
        out_specs=(pl.BlockSpec(memory_space=pl.ANY),) * 3,
        scratch_shapes=[
            pltpu.VMEM((REQ, LOC), F32),
            pltpu.VMEM((REQ, LOC), F32),
            pltpu.VMEM((2, REQ * 8, 128), F32),
            pltpu.VMEM((REQ, LOC), BF16),
            pltpu.VMEM((3, REQ, LOC), BF16),
            pltpu.VMEM((REQ, N, LOC), BF16),
            pltpu.SemaphoreType.DMA((CHUNKS + 2,)),
        ],
        compiler_params=pltpu.CompilerParams(vmem_limit_bytes=24 * 2**20),
    )(
        act,
        mixed,
        step_raw,
        bc_raw.reshape(2 * N, REQ),
        dt_norm_gain.reshape(1, DT_RANK),
        b_norm_gain.reshape(1, N),
        c_norm_gain.reshape(1, N),
        dt_weight,
        dt_bias.reshape(1, LOC),
        decay_log,
        skip_gain.reshape(1, LOC),
        conv_state.transpose(1, 0, 2),
        ssm_state,
    )
    return (output, next_conv.transpose(1, 0, 2), next_state)


def solution(mesh):
    return jax.shard_map(
        local,
        mesh=mesh,
        in_specs=(
            P("req", "chan"),
            P("chan"),
            P(None, None, "chan"),
            P(None, "chan"),
            P("chan"),
            P("chan", None),
            P(),
            P(),
            P(),
            P(None, "chan"),
            P("chan"),
            P(None, "chan"),
            P("chan"),
            P("req", None, "chan"),
            P("req", None, "chan"),
        ),
        out_specs=(P("req", "chan"), P("req", None, "chan"), P("req", None, "chan")),
        check_vma=False,
    )
```

```python
import jax
import jax.numpy as jnp
from jax import lax
from jax.experimental import pallas as pl
from jax.experimental.pallas import tpu as pltpu
from jax.sharding import PartitionSpec as P

D = 8192
N = 16
DT_RANK = 512
ZS = 8
XS = 4
DEVS = 32
REQ = 128
LOC = 256
MESH = pl.DeviceIdType.MESH
F32 = jnp.float32
BF16 = jnp.bfloat16

GREETED = ((-2, 0), (0, 2), (2, 0), (-1, 0), (0, -1), (0, 1), (1, 0))
OWN = (
    (1, -1, 0), (0, 2, 0), (1, 0, -1), (1, 0, 1), (0, 0, -1), (0, 0, 1), (0, -2, 0), (0, 0, 2), (1, -2, 0),
    (1, 0, 2), (1, 1, 0), (0, 1, 0), (1, 2, 0),
)
PASSES = (
    ((1, -1, 0), ((-2, 0), (0, -1), (0, 1))), ((1, 0, -1), ((1, 0), )),
    ((0, 2, 0), ((0, 2), (1, 0), (0, -1), (0, 1))), ((0, 0, -1), ((1, 0), )), ((0, 0, 1), ((-1, 0), )),
    ((1, 1, 0), ((0, 1), )), ((0, -2, 0), ((-1, 0), (0, -1), (-2, 0), (0, 2))), ((0, 1, 0), ((0, 1), )),
    ((1, 0, 2), ((2, 0), )), ((1, 0, 1), ()), ((1, -2, 0), ((0, -1), )), ((1, 2, 0), ((1, 0), )),
    ((1, -1, -1), ((0, -1), )), ((1, -1, 1), ((-1, 0), )), ((1, 1, -1), ((1, 0), )),
    ((1, -3, 0), ((0, 1), (0, -1), (-1, 0))), ((0, 0, 2), ()), ((0, 3, 0), ((0, 1), (0, -1))),
    ((0, -1, 1), ((0, 1), (-1, 0), (0, -1))), ((0, 2, 2), ((1, 0), (-1, 0))), ((0, -3, 0), ((0, 1), )),
    ((0, -2, -1), ((-1, 0), (1, 0))), ((1, 1, 1), ((0, 1), (1, 0))), ((0, 2, -1), ()), ((1, -2, -1), ((0, -1), )),
    ((0, 2, 1), ()), ((1, 2, 2), ((1, 0), )), ((0, 4, 0), ((0, 1), (0, -1))), ((0, -2, 2), ((-1, 0), )),
    ((0, 1, -1), ()), ((1, 3, 0), ((0, 1), )), ((1, -3, 1), ((0, 1), (-1, 0))), ((1, 2, -1), ((1, 0), )),
    ((0, 1, 1), ()), ((1, 4, 0), ((0, 2), )), ((1, -3, -1), ((-1, 0), )), ((0, 3, 2), ((1, 0), )), ((1, -2, 1), ()),
    ((1, -1, 2), ()), ((0, 3, 1), ()), ((0, -2, 1), ()), ((0, 3, -1), ()), ((0, -1, 2), ()), ((0, -1, -1), ()),
    ((0, 1, 2), ()), ((0, -1, 0), ()), ((0, -3, 1), ()), ((1, 2, 1), ()), ((0, -3, -1), ()), ((1, -2, 2), ()),
    ((1, 1, 2), ()), ((1, 3, 2), ()), ((0, -3, 2), ()), ((0, 4, -1), ()), ((0, 4, 1), ()), ((1, 4, 1), ()),
    ((1, 3, -1), ()), ((1, 3, 1), ()), ((1, 4, -1), ()), ((0, 4, 2), ()), ((1, 4, 2), ()), ((1, -3, 2), ()),
)


PEERS = sorted(
    [(z, x) for z in range(-3, 5) for x in range(-1, 3) if (z, x) != (0, 0)],
    key=lambda move: -abs(move[0]) - abs(move[1]),
)


def gather_kernel(
    hidden_hbm, gain_hbm, weight_hbm, conv_weight_hbm, conv_bias_hbm, proj_hbm, conv_state_hbm,
    act_out, mixed_out, step_out, bc_out,
    hidden, gain, conv_weight, conv_bias, proj, conv_state, raw, wide, ready, units, total, squares_x, squares_z, inverse, window, part, part_bc, got, got_bc,
    in_sem, weight_sem, recv_sem, send_sem, sq_sem, sum_sem, out_sem,
):
    req = lax.axis_index("req")
    me = lax.axis_index("chan")
    mz = me // XS
    mx = lax.rem(me, XS)

    def place(dz, dx):
        return lax.rem(mz + dz + ZS, ZS) * XS + lax.rem(mx + dx + XS, XS)

    small_copies = [
        pltpu.make_async_copy(source, target, in_sem.at[i])
        for i, (source, target) in enumerate(
            (
                (hidden_hbm, hidden),
                (gain_hbm, gain),
                (conv_weight_hbm, conv_weight),
                (conv_bias_hbm, conv_bias),
                (proj_hbm, proj),
                (conv_state_hbm, conv_state),
            )
        )
    ]
    small_copies[0].start()
    small_copies[1].start()
    weight_copies = [
        pltpu.make_async_copy(
            weight_hbm.at[pl.ds(i * 4096, 4096)], raw.at[pl.ds(i * 4096, 4096)], weight_sem.at[i]
        )
        for i in range(8)
    ]
    barrier = pltpu.get_barrier_semaphore()
    for hz, hx in GREETED:
        pl.semaphore_signal(barrier, inc=1, device_id=(req, place(-hz, -hx)), device_id_type=MESH)

    for copy in weight_copies:
        copy.start()
    for copy in small_copies[2:]:
        copy.start()
    small_copies[0].wait()
    small_copies[1].wait()
    widened = hidden[...].astype(F32)
    gain_rows = gain[...].astype(F32)
    for half in range(2):
        scaled = widened[:, half * 128 : half * 128 + 128] * gain_rows[half : half + 1]
        units[half, pl.ds(me, 1)] = scaled.astype(BF16)[None]
    square_row = lax.dot_general(
        jnp.ones((8, LOC), F32), widened * widened, (((1,), (1,)), ((), ())),
        precision=lax.Precision.HIGHEST, preferred_element_type=F32,
    )
    squares_x[pl.ds(mx, 1)] = square_row[None, :1]

    pl.semaphore_wait(barrier, len(GREETED))

    def push(half, z, x, hz, hx):
        owner = place(-z, -x)
        pltpu.make_async_remote_copy(
            units.at[half, owner], units.at[half, owner], send_sem.at[half],
            recv_sem.at[half, (z + hz) % ZS, (x + hx) % XS],
            device_id=(req, place(hz, hx)), device_id_type=MESH,
        ).start()

    def await_unit(half, z, x):
        owner = place(-z, -x)
        pltpu.make_async_copy(
            units.at[half, owner], units.at[half, owner], recv_sem.at[half, z % ZS, x % XS]
        ).wait()

    for half, hz, hx in OWN:
        push(half, 0, 0, hz, hx)
    for dx in (1, -1, 2):
        pltpu.make_async_remote_copy(
            squares_x.at[mx], squares_x.at[mx], sq_sem.at[0], sq_sem.at[1],
            device_id=(req, place(0, dx)), device_id_type=MESH,
        ).start()

    def convert(index, _):
        wide[...] = raw[pl.ds(pl.multiple_of(index * 1024, 1024), 1024), :].astype(F32)
        for side in range(2):
            for tile in range(2):
                column = side * 256 + tile * 128
                ready[pl.ds(pl.multiple_of(index * 256, 256), 256), column : column + 128] = wide[
                    pl.ds(2 * tile + side, 256, stride=4), :
                ].astype(BF16)
        return 0

    def multiply(z, x, first=False):
        owner = place(-z, -x)
        left = jnp.concatenate([units[0, owner], units[1, owner]], axis=1)
        product = jnp.dot(
            left, ready[pl.ds(pl.multiple_of(owner * 256, 256), 256), :], preferred_element_type=F32
        )
        total[...] = product if first else total[...] + product

    converted = 0

    def convert_to(count):
        nonlocal converted
        while converted < count:
            if converted % 4 == 0:
                weight_copies[converted // 4].wait()
            last = min(count, converted // 4 * 4 + 4)
            lax.fori_loop(converted, last, convert, 0)
            converted = last

    def settle():
        for copy in small_copies[2:]:
            copy.wait()
        pltpu.make_async_copy(
            squares_z.at[pl.ds(0, 7)], squares_z.at[pl.ds(0, 7)], sq_sem.at[3]
        ).wait()
        inverse_row = lax.rsqrt(jnp.sum(squares_z[...], axis=0) / D + 1e-05)
        inverse[...] = jnp.transpose(jnp.broadcast_to(inverse_row, (128, 128)))
        older = conv_state[0].astype(F32) * conv_weight[0:1]
        older += conv_state[1].astype(F32) * conv_weight[1:2]
        window[...] = older + conv_state[2].astype(F32) * conv_weight[2:3]

    convert_to(8)
    arrived = {}
    pending = []
    started = False
    column = {0}
    for step, ((half, z, x), moves) in enumerate(PASSES):
        await_unit(half, z, x)
        for hz, hx in moves:
            push(half, z, x, hz, hx)
        arrived[(z, x)] = arrived.get((z, x), 0) + 1
        if arrived[(z, x)] == 2:
            pending.append((z, x))
        if x == 0 and z not in column:
            column.add(z)
            if len(column) == ZS:
                pltpu.make_async_copy(
                    squares_x.at[pl.ds(0, 3)], squares_x.at[pl.ds(0, 3)], sq_sem.at[1]
                ).wait()
                squares_z[pl.ds(mz, 1)] = jnp.sum(squares_x[...], axis=0, keepdims=True)
                for hz in (1, -1, 2, -2, 3, -3, 4):
                    pltpu.make_async_remote_copy(
                        squares_z.at[mz], squares_z.at[mz], sq_sem.at[2], sq_sem.at[3],
                        device_id=(req, place(hz, 0)), device_id_type=MESH,
                    ).start()
        if converted < DEVS:
            convert_to(min(DEVS, converted + 2))
        elif pending:
            if not started:
                multiply(0, 0, True)
                started = True
            multiply(*pending.pop(0))
        if step == len(PASSES) - 5:
            settle()
    while pending:
        multiply(*pending.pop(0))

    mixed = [
        (total[:, i * 128 : i * 128 + 128] * inverse[...]).astype(BF16) for i in range(4)
    ]
    new_inputs = jnp.concatenate(mixed[:2], axis=1)
    mixed_out[...] = jnp.concatenate(mixed, axis=1)
    summed = window[...] + new_inputs.astype(F32) * conv_weight[3:4] + conv_bias[...]
    act = (summed * jax.nn.sigmoid(summed)).astype(BF16)
    act_out[...] = act
    projected = lax.dot_general(
        proj[...], act, (((1,), (1,)), ((), ())), preferred_element_type=F32
    )
    part[...] = projected[:DT_RANK].astype(BF16)
    for i in range(2 * N):
        part_bc[i] = projected[DT_RANK + i : DT_RANK + i + 1]

    def rows(index):
        return pl.ds(pl.multiple_of(index * 16, 16), 16)

    for hz, hx in PEERS:
        peer = place(hz, hx)
        pltpu.make_async_remote_copy(
            part.at[rows(peer)], got.at[rows(me)], sum_sem.at[0], sum_sem.at[1],
            device_id=(req, peer), device_id_type=MESH,
        ).start()
        pltpu.make_async_remote_copy(
            part_bc.at[peer], got_bc.at[me], sum_sem.at[2], sum_sem.at[3],
            device_id=(req, peer), device_id_type=MESH,
        ).start()
    got[rows(me), :] = part[rows(me), :]
    got_bc[pl.ds(me, 1)] = part_bc[pl.ds(me, 1)]

    some, some_bc = pl.ds(0, 31 * 16), pl.ds(0, 31)
    pltpu.make_async_copy(got.at[some], got.at[some], sum_sem.at[1]).wait()
    pltpu.make_async_copy(got_bc.at[some_bc], got_bc.at[some_bc], sum_sem.at[3]).wait()
    reduced = got[0:16].astype(F32)
    for i in range(1, DEVS):
        reduced += got[i * 16 : i * 16 + 16].astype(F32)
    step_out[rows(me), :] = reduced.astype(BF16)
    bc_out[pl.ds(me, 1)] = jnp.sum(got_bc[...], axis=0, keepdims=True)

    for hz, hx in PEERS:
        peer = place(hz, hx)
        pltpu.make_async_remote_copy(
            step_out.at[rows(me)], step_out.at[rows(me)], out_sem.at[0], out_sem.at[1],
            device_id=(req, peer), device_id_type=MESH,
        ).start()
        pltpu.make_async_remote_copy(
            bc_out.at[me], bc_out.at[me], out_sem.at[2], out_sem.at[3],
            device_id=(req, peer), device_id_type=MESH,
        ).start()
    for half in range(2):
        pltpu.make_async_copy(
            units.at[half, pl.ds(0, 31)], units.at[half, pl.ds(0, 31)], send_sem.at[half]
        ).wait()
    pltpu.make_async_copy(squares_x.at[pl.ds(0, 3)], squares_x.at[pl.ds(0, 3)], sq_sem.at[0]).wait()
    pltpu.make_async_copy(squares_z.at[pl.ds(0, 7)], squares_z.at[pl.ds(0, 7)], sq_sem.at[2]).wait()
    for i in (0, 2):
        pltpu.make_async_copy(
            (got if i == 0 else got_bc).at[some if i == 0 else some_bc],
            (got if i == 0 else got_bc).at[some if i == 0 else some_bc],
            sum_sem.at[i],
        ).wait()
    for i in range(4):
        ref, span = (step_out, some) if i < 2 else (bc_out, some_bc)
        pltpu.make_async_copy(ref.at[span], ref.at[span], out_sem.at[i]).wait()


def front(hidden, norm_gain, in_weight, conv_weight, conv_bias, x_proj_weight, conv_state):
    weight = in_weight.reshape(D, 2, 2, 128).transpose(0, 2, 1, 3).reshape(4 * D, 128)
    vmem = pl.BlockSpec(memory_space=pltpu.VMEM)
    return pl.pallas_call(
        gather_kernel,
        out_shape=(
            pltpu.VMEM((REQ, LOC), BF16),
            pltpu.VMEM((REQ, 2 * LOC), BF16),
            pltpu.VMEM((DT_RANK, REQ), BF16),
            pltpu.VMEM((2 * N, 1, REQ), F32),
        ),
        in_specs=[pl.BlockSpec(memory_space=pltpu.HBM)] * 7,
        out_specs=(vmem,) * 4,
        scratch_shapes=[
            pltpu.VMEM((REQ, LOC), BF16),
            pltpu.VMEM((2, 128), BF16),
            pltpu.VMEM((4, LOC), F32),
            pltpu.VMEM((1, LOC), F32),
            pltpu.VMEM((DT_RANK + 2 * N, LOC), BF16),
            pltpu.VMEM((3, REQ, LOC), BF16),
            pltpu.VMEM((4 * D, 128), BF16),
            pltpu.VMEM((1024, 128), F32),
            pltpu.VMEM((D, 2 * LOC), BF16),
            pltpu.VMEM((2, DEVS, REQ, 128), BF16),
            pltpu.VMEM((REQ, 2 * LOC), F32),
            pltpu.VMEM((XS, 1, REQ), F32),
            pltpu.VMEM((ZS, 1, REQ), F32),
            pltpu.VMEM((128, 128), F32),
            pltpu.VMEM((REQ, LOC), F32),
            pltpu.VMEM((DT_RANK, REQ), BF16),
            pltpu.VMEM((2 * N, 1, REQ), F32),
            pltpu.VMEM((DT_RANK, REQ), BF16),
            pltpu.VMEM((DEVS, 1, REQ), F32),
            pltpu.SemaphoreType.DMA((6,)),
            pltpu.SemaphoreType.DMA((8,)),
            pltpu.SemaphoreType.DMA((2, ZS, XS)),
            pltpu.SemaphoreType.DMA((2,)),
            pltpu.SemaphoreType.DMA((4,)),
            pltpu.SemaphoreType.DMA((4,)),
            pltpu.SemaphoreType.DMA((4,)),
        ],
        compiler_params=pltpu.CompilerParams(
            collective_id=0, has_side_effects=True, vmem_limit_bytes=56 * 2**20
        ),
    )(
        hidden,
        norm_gain.reshape(2, 128),
        weight,
        conv_weight,
        conv_bias.reshape(1, LOC),
        x_proj_weight.T,
        conv_state.transpose(1, 0, 2),
    )


CHUNKS = 8
ROWS = REQ // CHUNKS


def state_kernel(
    act, mixed, step_raw, bc_raw, dt_gain, b_gain, c_gain, dt_weight, dt_bias, decay_log, skip_gain, conv_state, state,
    out_hbm, next_conv_hbm, next_state_hbm,
    step_size, drive, folded, out, next_conv, next_state, sem,
):
    next_conv[0:2] = conv_state[1:3]
    next_conv[2] = mixed[:, :LOC]
    conv_copy = pltpu.make_async_copy(next_conv, next_conv_hbm, sem.at[CHUNKS])
    conv_copy.start()
    raw = step_raw[...].astype(F32)
    scale = lax.rsqrt(jnp.mean(raw * raw, axis=0, keepdims=True) + 1e-06)
    normed = (jnp.transpose(raw * scale) * dt_gain[...]).astype(BF16)
    before = jnp.dot(normed, dt_weight[...], preferred_element_type=F32) + dt_bias[...]
    size = jnp.maximum(before, 0.0) + jnp.log1p(jnp.exp(-jnp.abs(before)))
    step_size[...] = size
    drive[...] = size * act[...].astype(F32)
    square = (N, N)
    eye = lax.broadcasted_iota(jnp.int32, square, 0) == lax.broadcasted_iota(jnp.int32, square, 1)
    turned = []
    for part, gain_row in ((0, b_gain), (N, c_gain)):
        column = jnp.sum(
            jnp.where(eye, jnp.broadcast_to(gain_row[...], square), 0.0), axis=1, keepdims=True
        )
        values = bc_raw[part : part + N]
        scale = lax.rsqrt(jnp.mean(values * values, axis=0, keepdims=True) + 1e-06)
        turned.append(values * scale * column)
    b_turned, c_turned = turned
    rates = -jnp.exp(decay_log[...])
    copies = [conv_copy]
    for chunk in range(CHUNKS):
        rows = slice(chunk * ROWS, chunk * ROWS + ROWS)
        for r in range(chunk * ROWS, chunk * ROWS + ROWS):
            decay = jnp.exp(step_size[r : r + 1, :] * rates)
            new = decay * state[r].astype(F32) + drive[r : r + 1, :] * b_turned[:, r : r + 1]
            next_state[r] = new.astype(BF16)
            weighted = new * c_turned[:, r : r + 1]
            for tile in range(2):
                lanes = slice(tile * 128, tile * 128 + 128)
                folded[tile, r * 8 : r * 8 + 8] = weighted[:8, lanes] + weighted[8:, lanes]
        copies.append(
            pltpu.make_async_copy(next_state.at[rows], next_state_hbm.at[rows], sem.at[chunk])
        )
        copies[-1].start()
        first = chunk * ROWS * 8
        halves = []
        for tile in range(2):
            half = folded[tile, pl.ds(first, ROWS, stride=8), :]
            for i in range(1, 8):
                half += folded[tile, pl.ds(first + i, ROWS, stride=8), :]
            halves.append(half)
        summed = jnp.concatenate(halves, axis=1)
        act_wide = act[rows, :].astype(F32)
        gate = mixed[rows, LOC:].astype(F32)
        gated = (summed + skip_gain[...] * act_wide) * (gate * jax.nn.sigmoid(gate))
        out[rows, :] = gated.astype(BF16)
    copies.append(pltpu.make_async_copy(out, out_hbm, sem.at[CHUNKS + 1]))
    copies[-1].start()
    for copy in copies:
        copy.wait()


def local(
    hidden,
    norm_gain,
    in_weight,
    conv_weight,
    conv_bias,
    x_proj_weight,
    dt_norm_gain,
    b_norm_gain,
    c_norm_gain,
    dt_weight,
    dt_bias,
    decay_log,
    skip_gain,
    conv_state,
    ssm_state,
):
    act, mixed, step_raw, bc_raw = front(
        hidden, norm_gain, in_weight, conv_weight, conv_bias, x_proj_weight, conv_state
    )
    whole = pl.BlockSpec(memory_space=pltpu.VMEM)
    output, next_conv, next_state = pl.pallas_call(
        state_kernel,
        out_shape=(
            jax.ShapeDtypeStruct((REQ, LOC), BF16),
            jax.ShapeDtypeStruct((3, REQ, LOC), BF16),
            jax.ShapeDtypeStruct((REQ, N, LOC), BF16),
        ),
        in_specs=[whole] * 13,
        out_specs=(pl.BlockSpec(memory_space=pl.ANY),) * 3,
        scratch_shapes=[
            pltpu.VMEM((REQ, LOC), F32),
            pltpu.VMEM((REQ, LOC), F32),
            pltpu.VMEM((2, REQ * 8, 128), F32),
            pltpu.VMEM((REQ, LOC), BF16),
            pltpu.VMEM((3, REQ, LOC), BF16),
            pltpu.VMEM((REQ, N, LOC), BF16),
            pltpu.SemaphoreType.DMA((CHUNKS + 2,)),
        ],
        compiler_params=pltpu.CompilerParams(vmem_limit_bytes=24 * 2**20),
    )(
        act,
        mixed,
        step_raw,
        bc_raw.reshape(2 * N, REQ),
        dt_norm_gain.reshape(1, DT_RANK),
        b_norm_gain.reshape(1, N),
        c_norm_gain.reshape(1, N),
        dt_weight,
        dt_bias.reshape(1, LOC),
        decay_log,
        skip_gain.reshape(1, LOC),
        conv_state.transpose(1, 0, 2),
        ssm_state,
    )
    return (output, next_conv.transpose(1, 0, 2), next_state)


def solution(mesh):
    return jax.shard_map(
        local,
        mesh=mesh,
        in_specs=(
            P("req", "chan"),
            P("chan"),
            P(None, None, "chan"),
            P(None, "chan"),
            P("chan"),
            P("chan", None),
            P(),
            P(),
            P(),
            P(None, "chan"),
            P("chan"),
            P(None, "chan"),
            P("chan"),
            P("req", None, "chan"),
            P("req", None, "chan"),
        ),
        out_specs=(P("req", "chan"), P("req", None, "chan"), P("req", None, "chan")),
        check_vma=False,
    )
```
